512 devices in a mesh: chan: 8 (over y_hi, x), row: 64 (over z, y_lo, core).
Axes of the slice: x: 4, y: 8 (y_hi: 2, y_lo: 4; y = y_hi * 4 + y_lo), z: 8, core: 2. Of those that a mesh axis runs over, the one named last changes fastest.
Arguments:
- inputs: bfloat16 [1, 192, 448, 1024], P(None, 'row', None, 'chan'), may hold values from -6 to 6
- cotangent: bfloat16 [1, 192, 448, 1024], P(None, 'row', None, 'chan'), may hold values from -6 to 6
- ln_gain: float32 [1024], P('chan'), may hold values from 0.1 to 1.9
- ln_shift: float32 [1024], P('chan'), may hold values from -3 to 3
- first_weight: bfloat16 [2, 1024, 128], P(None, 'chan'), may hold values from -0.375 to 0.375
- first_bias: float32 [2, 1024], P(None, 'chan'), may hold values from -3 to 3
- second_weight: bfloat16 [2, 1024, 128], P(None, 'chan'), may hold values from -0.375 to 0.375
- second_bias: float32 [2, 1024], P(None, 'chan'), may hold values from -3 to 3
Outputs:
- input_grad: bfloat16 [1, 192, 448, 1024], P(None, 'row', None, 'chan')
- first_weight_grad: float32 [2, 1024, 128], P(None, 'chan')
- first_bias_grad: float32 [2, 1024], P(None, 'chan')
- second_weight_grad: float32 [2, 1024, 128], P(None, 'chan')
- second_bias_grad: float32 [2, 1024], P(None, 'chan')
- gain_grad: float32 [1024], P('chan')
- shift_grad: float32 [1024], P('chan')
The draws below stay inside these ranges and needn't reach their ends.
All inputs are finite; a program needn't handle non-finite values.
Results may differ from the reference program's by a relative error of at most 0.03.
The reference program's roundings to bfloat16 on the way count: a program that leaves them out, or rounds other values in their place, can miss the bound.
Values sent between devices are 32-bit elements; how exact they have to be, the bound alone decides.
A program may use at most 64 MiB of HBM per device.

```python
import math
import jax
import jax.numpy as jnp
from jax import lax

BATCH = 1
H = 192
W = 448
K = 192
NB = 8
BS = 128
C = 1024


def levels(own_key, extent, pieces, low, high):
    def one(dim, blocks):
        steps = jax.random.uniform(jax.random.fold_in(jax.random.fold_in(own_key, 6), dim), (blocks,), jnp.float32, low / len(pieces), high / len(pieces))
        return jnp.repeat(jnp.exp(steps), extent[dim] // blocks).reshape((-1,) + (1,) * (len(extent) - dim - 1))

    loudness = one(*pieces[0])
    for cut in pieces[1:]:
        loudness = loudness * one(*cut)
    return loudness


def bell_draw(rng, dims, scale, reach, shards=(), kind=jnp.bfloat16):
    array = scale * jax.random.normal(rng, dims, jnp.float32)
    if shards:
        array = array * levels(rng, dims, shards, -0.22, 0.18)
    return jnp.clip(array, -reach, reach).astype(kind)


def setup_inputs(seed: int = 0) -> dict:
    key_of = jax.random.split(jax.random.key(seed), 9)
    inputs = bell_draw(key_of[0], (BATCH, H, W, C), 1.0, 6.0, ((1, 64), (3, 8)))
    cotangent = bell_draw(key_of[1], (BATCH, H, W, C), 1.0, 6.0, ((1, 64), (3, 8)))
    ln_gain = jnp.clip(1.0 + 0.18 * jax.random.normal(key_of[2], (C,), jnp.float32), 0.1, 1.9)
    ln_shift = bell_draw(key_of[3], (C,), 0.5, 3.0, ((0, 8),), jnp.float32)
    first_weight = bell_draw(key_of[4], (2, C, BS), (2 * BS) ** -0.5, 0.375, ((1, 8),))
    first_bias = bell_draw(key_of[5], (2, C), 0.5, 3.0, ((1, 8),), jnp.float32)
    second_weight = bell_draw(key_of[6], (2, C, BS), (2 * BS) ** -0.5, 0.375, ((1, 8),))
    second_bias = bell_draw(key_of[7], (2, C), 0.5, 3.0, ((1, 8),), jnp.float32)
    return {"inputs": inputs, "cotangent": cotangent, "ln_gain": ln_gain, "ln_shift": ln_shift, "first_weight": first_weight, "first_bias": first_bias, "second_weight": second_weight, "second_bias": second_bias}


EPS = 1e-05
LAMBDA = 0.01
ROOT_TWO_PI = math.sqrt(2.0 / math.pi)

def gelu_parts(values):
    inner = ROOT_TWO_PI * (values + 0.044715 * values * values * values)
    tangent = jnp.tanh(inner)
    output = 0.5 * values * (1.0 + tangent)
    slope = 0.5 * (1.0 + tangent) + 0.5 * values * (1.0 - tangent * tangent) * ROOT_TWO_PI * (1.0 + 3.0 * 0.044715 * values * values)
    return (output, slope)

def shrink_slope(values):
    tangent = jnp.tanh(values / LAMBDA)
    return tangent * tangent

def mult(left, right):
    return jnp.einsum('gkni,nio->gkno', left.astype(jnp.float32), right)

def mult_t(left, right):
    return jnp.einsum('gkno,nio->gkni', left.astype(jnp.float32), right)

def outer(left, right):
    return jnp.einsum('gkni,gkno->nio', left.astype(jnp.float32), right.astype(jnp.float32))

def rounded(values):
    return lax.optimization_barrier(values.astype(jnp.bfloat16))

def reference(inputs, cotangent, ln_gain, ln_shift, first_weight, first_bias, second_weight, second_bias):
    w_one = first_weight.astype(jnp.float32).reshape(2, NB, BS, BS)
    w_two = second_weight.astype(jnp.float32).reshape(2, NB, BS, BS)
    b_one = first_bias.reshape(2, NB, BS)
    b_two = second_bias.reshape(2, NB, BS)
    kept = jnp.where(jnp.arange(K) == 0, 1.0, 2.0).astype(jnp.float32)
    dw_one = jnp.zeros((2, NB, BS, BS), jnp.float32)
    dw_two = jnp.zeros((2, NB, BS, BS), jnp.float32)
    db_one = jnp.zeros((2, NB, BS), jnp.float32)
    db_two = jnp.zeros((2, NB, BS), jnp.float32)
    gain_sum = jnp.zeros((C,), jnp.float32)
    shift_sum = jnp.zeros((C,), jnp.float32)
    grads = []
    for sample in range(BATCH):
        values = inputs[sample].astype(jnp.float32)
        mean = lax.optimization_barrier(jnp.mean(values, -1, keepdims=True))
        centred = values - mean
        variance = lax.optimization_barrier(jnp.mean(centred * centred, -1, keepdims=True))
        rstd = lax.rsqrt(variance + EPS)
        normed = centred * rstd
        mixed_in = normed * ln_gain + ln_shift
        spectrum = jnp.fft.fft(jnp.fft.rfft(mixed_in, axis=1, norm='ortho')[:, :K, :], axis=0, norm='ortho')
        spec_re = rounded(spectrum.real).reshape(H, K, NB, BS)
        spec_im = rounded(spectrum.imag).reshape(H, K, NB, BS)
        pre_one_re = mult(spec_re, w_one[0]) - mult(spec_im, w_one[1]) + b_one[0]
        pre_one_im = mult(spec_re, w_one[1]) + mult(spec_im, w_one[0]) + b_one[1]
        act_re, slope_re = gelu_parts(pre_one_re)
        act_im, slope_im = gelu_parts(pre_one_im)
        hid_re = rounded(act_re)
        hid_im = rounded(act_im)
        pre_two_re = mult(hid_re, w_two[0]) - mult(hid_im, w_two[1]) + b_two[0]
        pre_two_im = mult(hid_re, w_two[1]) + mult(hid_im, w_two[0]) + b_two[1]
        cot_values = cotangent[sample].astype(jnp.float32)
        cot_lon = jnp.fft.rfft(cot_values, axis=1, norm='ortho')[:, :K, :] * kept[None, :, None]
        cot_spec = jnp.fft.fft(cot_lon, axis=0, norm='ortho')
        cot_re = cot_spec.real.reshape(H, K, NB, BS)
        cot_im = cot_spec.imag.reshape(H, K, NB, BS)
        grad_two_re = rounded(cot_re * shrink_slope(pre_two_re))
        grad_two_im = rounded(cot_im * shrink_slope(pre_two_im))
        grad_hid_re = mult_t(grad_two_re, w_two[0]) + mult_t(grad_two_im, w_two[1])
        grad_hid_im = mult_t(grad_two_im, w_two[0]) - mult_t(grad_two_re, w_two[1])
        dw_two = dw_two + jnp.stack([outer(hid_re, grad_two_re) + outer(hid_im, grad_two_im), outer(hid_re, grad_two_im) - outer(hid_im, grad_two_re)])
        db_two = db_two + jnp.stack([lax.optimization_barrier(jnp.sum(grad_two_re.astype(jnp.float32), (0, 1))), lax.optimization_barrier(jnp.sum(grad_two_im.astype(jnp.float32), (0, 1)))])
        grad_pre_re = rounded(grad_hid_re * slope_re)
        grad_pre_im = rounded(grad_hid_im * slope_im)
        dw_one = dw_one + jnp.stack([outer(spec_re, grad_pre_re) + outer(spec_im, grad_pre_im), outer(spec_re, grad_pre_im) - outer(spec_im, grad_pre_re)])
        db_one = db_one + jnp.stack([lax.optimization_barrier(jnp.sum(grad_pre_re.astype(jnp.float32), (0, 1))), lax.optimization_barrier(jnp.sum(grad_pre_im.astype(jnp.float32), (0, 1)))])
        grad_spec_re = mult_t(grad_pre_re, w_one[0]) + mult_t(grad_pre_im, w_one[1])
        grad_spec_im = mult_t(grad_pre_im, w_one[0]) - mult_t(grad_pre_re, w_one[1])
        grad_spec = lax.complex(grad_spec_re.reshape(H, K, C), grad_spec_im.reshape(H, K, C))
        grad_lon = jnp.fft.ifft(grad_spec, axis=0, norm='ortho') / kept[None, :, None]
        padded = jnp.pad(grad_lon, ((0, 0), (0, W // 2 + 1 - K), (0, 0)))
        grad_mixed = jnp.fft.irfft(padded, n=W, axis=1, norm='ortho')
        grad_norm = grad_mixed * ln_gain
        mean_one = lax.optimization_barrier(jnp.mean(grad_norm, -1, keepdims=True))
        mean_two = lax.optimization_barrier(jnp.mean(grad_norm * normed, -1, keepdims=True))
        input_part = cot_values + rstd * (grad_norm - mean_one - normed * mean_two)
        grads.append(input_part.astype(jnp.bfloat16))
        gain_sum = gain_sum + lax.optimization_barrier(jnp.sum(grad_mixed * normed, (0, 1)))
        shift_sum = shift_sum + lax.optimization_barrier(jnp.sum(grad_mixed, (0, 1)))
    spec_scale = 1.0 / (BATCH * H * K) ** 0.5
    ln_scale = 1.0 / (BATCH * H * W) ** 0.5
    return (jnp.stack(grads), (dw_one * spec_scale).reshape(2, C, BS), (db_one * spec_scale).reshape(2, C), (dw_two * spec_scale).reshape(2, C, BS), (db_two * spec_scale).reshape(2, C), gain_sum * ln_scale, shift_sum * ln_scale)
```

```python
import functools
import math

import jax
import jax.numpy as jnp
import ml_dtypes
import numpy as np
from jax import lax
from jax.experimental import pallas as pl
from jax.experimental.pallas import tpu as pltpu
from jax.sharding import PartitionSpec as P

H = 192
W = 448
K = 192
BS = 128
C = 1024
ROWS = 64
CHANS = 8
HL = H // ROWS
KL = K // ROWS
CHUNK = 2 * HL * KL
LINES = ROWS * CHUNK
PIECE = 9
GLINES = ROWS * PIECE
WPAD = 512

EPS = 1e-05
LAMBDA = 0.01
ROOT_TWO_PI = math.sqrt(2.0 / math.pi)
F32 = jnp.float32
BF16 = jnp.bfloat16
MESH = pl.DeviceIdType.MESH


def halves(table):
    table = table.astype(np.float32)
    high = table.astype(ml_dtypes.bfloat16)
    low = (table - high.astype(np.float32)).astype(ml_dtypes.bfloat16)
    return np.stack([high, low])


def lon_table():
    number = np.arange(K).reshape(ROWS, 1, KL)
    part = np.arange(2).reshape(1, 2, 1)
    number, part = np.broadcast_arrays(number, part)
    number, part = number.reshape(-1, 1), part.reshape(-1, 1)
    phase = (number * np.arange(W)[None, :] % W) * (2.0 * math.pi / W)
    return np.where(part == 0, np.cos(phase), -np.sin(phase)) / math.sqrt(W)


def lat_table():
    q = np.arange(2).reshape(2, 1, 1, 1, 1)
    g = np.arange(H).reshape(1, H, 1, 1, 1)
    hh = np.arange(HL).reshape(1, 1, HL, 1, 1)
    s = np.arange(ROWS).reshape(1, 1, 1, ROWS, 1)
    p = np.arange(2).reshape(1, 1, 1, 1, 2)
    phase = (g * (s * HL + hh) % H) * (2.0 * math.pi / H)
    cosine, sine = np.cos(phase), np.sin(phase)
    table = np.where(q == p, cosine, np.where(q == 0, sine, -sine)) / math.sqrt(H)
    return table.reshape(2 * H, HL * ROWS * 2)


def dot(a, b):
    return lax.dot_general(a, b, (((1,), (0,)), ((), ())), preferred_element_type=F32)


def dot_t(a, b):
    return lax.dot_general(a, b, (((1,), (1,)), ((), ())), preferred_element_type=F32)


def dot_c(a, b):
    return lax.dot_general(a, b, (((0,), (0,)), ((), ())), preferred_element_type=F32)


def split(values):
    high = values.astype(BF16)
    return high, (values - high.astype(F32)).astype(BF16)


def dot3(table, values):
    high, low = split(values)
    return dot(table[0], high) + (dot(table[1], high) + dot(table[0], low))


def gelu_parts(values):
    square = values * values
    tangent = jnp.tanh(ROOT_TWO_PI * (values + 0.044715 * (square * values)))
    plus = 0.5 * (1.0 + tangent)
    slope = plus + 0.5 * values * (1.0 - tangent * tangent) * (
        ROOT_TWO_PI * (1.0 + 3.0 * 0.044715 * square)
    )
    return values * plus, slope


def block_matrix(weight):
    real, imag = weight[0], weight[1]
    return jnp.concatenate(
        [jnp.concatenate([real, imag], 1), jnp.concatenate([-imag, real], 1)], 0
    )


def spread(stats, width):
    high = stats.astype(BF16).astype(F32)
    rest = stats - high
    mid = rest.astype(BF16).astype(F32)
    low = rest - mid
    pieces = jnp.concatenate([high, mid, low, jnp.zeros_like(high)], 0).astype(BF16)
    line = lax.broadcasted_iota(jnp.int32, (32, 2 * HL * BS), 0) % 8
    column = lax.broadcasted_iota(jnp.int32, (32, 2 * HL * BS), 1) // BS
    pick = (line == column).astype(F32).astype(BF16)
    return dot_c(pieces, pick)[:width]


def kernel(
    x_ref, cot_ref, gain_ref, shift_ref, w1_ref, b1_ref, w2_ref, b2_ref,
    lon_ref, lont_ref, lat_ref, latt_ref,
    out_ref, gw1_ref, gb1_ref, gw2_ref, gb2_ref, gg_ref, gs_ref,
    sc, rc, sx, rx, sg, rg, st, rt, su, ru, normed_ref, rstd_ref,
    spec_ref, nspec_ref, hid_ref, slope_ref, factor_ref, gtwo_ref, gpre_ref,
    gw, rw, fold, piece, aw,
    send_sem, recv_sem,
):
    chan = lax.axis_index("chan")
    row = lax.axis_index("row")

    barrier = pltpu.get_barrier_semaphore()

    def greet_row(j, carry):
        pl.semaphore_signal(
            barrier, inc=1, device_id={"row": lax.rem(row + j, ROWS)}, device_id_type=MESH
        )
        return carry

    def greet_chan(j, carry):
        pl.semaphore_signal(
            barrier, inc=1, device_id={"chan": lax.rem(chan + j, CHANS)}, device_id_type=MESH
        )
        return carry

    lax.fori_loop(1, CHANS, greet_chan, 0)
    lax.fori_loop(1, ROWS, greet_row, 0)

    def send_row(source, target, lines, which, same):
        def one(j, carry):
            other = lax.rem(row + j, ROWS)
            block = source if same else source.at[pl.ds(other * lines, lines)]
            pltpu.make_async_remote_copy(
                src_ref=block,
                dst_ref=target.at[pl.ds(row * lines, lines)],
                send_sem=send_sem.at[which],
                recv_sem=recv_sem.at[which],
                device_id={"row": other},
                device_id_type=MESH,
            ).start()
            return carry

        lax.fori_loop(1, ROWS, one, 0)
        own = pl.ds(row * lines, lines)
        pltpu.make_async_copy(
            source if same else source.at[own], target.at[own], recv_sem.at[which]
        ).start()

    def send_chan(source, target, which):
        def one(j, carry):
            pltpu.make_async_remote_copy(
                src_ref=source,
                dst_ref=target.at[chan],
                send_sem=send_sem.at[which],
                recv_sem=recv_sem.at[which],
                device_id={"chan": lax.rem(chan + j, CHANS)},
                device_id_type=MESH,
            ).start()
            return carry

        lax.fori_loop(1, CHANS, one, 0)
        pltpu.make_async_copy(source, target.at[chan], recv_sem.at[which]).start()

    def arrived(target, which):
        pltpu.make_async_copy(target, target, recv_sem.at[which]).wait()

    def left(target, which):
        pltpu.make_async_copy(target, target, send_sem.at[which]).wait()

    ones_wide = jnp.ones((BS, BS), F32).astype(BF16)
    ones_thin = jnp.ones((16, BS), F32).astype(BF16)

    st[...] = jnp.zeros_like(st)
    for h in range(HL):
        block = x_ref[0, h]
        average = dot(block, ones_wide) * (1.0 / BS)
        centred = block.astype(F32) - average
        high, low = split(centred * centred)
        st[h : h + 1, :W] = dot_t(ones_thin, block)[:1]
        st[HL + h : HL + h + 1, :W] = (dot_t(ones_thin, high) + dot_t(ones_thin, low))[:1]
    for h in range(HL):
        block = cot_ref[0, h]
        sc[pl.ds(h, 2 * K, stride=HL), :] = dot(lon_ref[0], block) + dot(lon_ref[1], block)

    pl.semaphore_wait(barrier, ROWS - 1 + CHANS - 1)
    send_chan(st, rt, 0)
    send_row(sc, rc, CHUNK, 1, False)

    arrived(rt, 0)
    total = rt[0]
    for c in range(1, CHANS):
        total = total + rt[c]
    mean = total[:HL] * (1.0 / C)
    squares = total[HL : 2 * HL]
    for c in range(CHANS):
        away = rt[c][:HL] * (1.0 / BS) - mean
        squares = squares + BS * (away * away)
    rstd = lax.rsqrt(squares * (1.0 / C) + EPS)
    wide = spread(jnp.concatenate([mean, rstd, jnp.zeros((2, WPAD), F32)], 0), W)
    for h in range(HL):
        centre = wide[:, h * BS : (h + 1) * BS]
        scale = wide[:, (HL + h) * BS : (HL + h + 1) * BS]
        normed = (x_ref[0, h].astype(F32) - centre) * scale
        normed_ref[h] = normed
        rstd_ref[h] = scale
        sx[pl.ds(h, 2 * K, stride=HL), :] = dot3(lon_ref, normed)
    send_row(sx, rx, CHUNK, 2, False)

    one_matrix = block_matrix(w1_ref)
    two_matrix = block_matrix(w2_ref)
    one_bias = jnp.concatenate([b1_ref[0:1], b1_ref[1:2]], 1)
    two_bias = jnp.concatenate([b2_ref[0:1], b2_ref[1:2]], 1)
    gain = gain_ref[...]
    gain_two = jnp.concatenate([gain, gain], 1)
    shift_two = jnp.concatenate([shift_ref[...] * math.sqrt(H * W), jnp.zeros((1, BS), F32)], 1)
    first = jnp.where(row == 0, 1.0, 0.0).astype(F32)

    def spectrum(landed):
        columns = []
        for k in range(KL):
            columns.append(
                jnp.concatenate(
                    [landed[pl.ds(k * HL + h, 2 * ROWS, stride=HL * KL), :] for h in range(HL)], 0
                )
            )
        return dot3(lat_ref, jnp.concatenate(columns, 1))

    def tokens(values, k):
        block = values[:, k * BS : (k + 1) * BS]
        return jnp.concatenate([block[:H], block[H:]], 1)

    arrived(rx, 2)
    spec = spectrum(rx)
    for k in range(KL):
        plain = tokens(spec, k)
        nspec_ref[k] = plain
        mixed = plain * gain_two
        if k == 0:
            line = lax.broadcasted_iota(jnp.int32, (H, 2 * BS), 0)
            mixed = mixed + jnp.where(line == 0, shift_two * first, 0.0)
        rounded = mixed.astype(BF16)
        spec_ref[k] = rounded
        act, slope = gelu_parts(dot(rounded, one_matrix) + one_bias)
        hidden = act.astype(BF16)
        hid_ref[k] = hidden
        slope_ref[k] = slope
        tangent = jnp.tanh((dot(hidden, two_matrix) + two_bias) / LAMBDA)
        factor_ref[k] = tangent * tangent

    arrived(rc, 1)
    cot_spec = spectrum(rc)
    gain_sum = jnp.zeros((1, 2 * BS), F32)
    one_sum = jnp.zeros((1, 2 * BS), F32)
    two_sum = jnp.zeros((1, 2 * BS), F32)
    columns = []
    for k in range(KL):
        cot_block = tokens(cot_spec, k) * (2.0 - first if k == 0 else 2.0)
        grad_two = (cot_block * factor_ref[k]).astype(BF16)
        gtwo_ref[k] = grad_two
        grad_pre = (dot_t(grad_two, two_matrix) * slope_ref[k]).astype(BF16)
        gpre_ref[k] = grad_pre
        grad_spec = dot_t(grad_pre, one_matrix)
        two_sum = two_sum + jnp.sum(grad_two.astype(F32), 0, keepdims=True)
        one_sum = one_sum + jnp.sum(grad_pre.astype(F32), 0, keepdims=True)
        gain_sum = gain_sum + jnp.sum(grad_spec * nspec_ref[k], 0, keepdims=True)
        if k == 0:
            shift_sum = grad_spec[0:1, :BS] * first
        columns.append(jnp.concatenate([grad_spec[:, :BS], grad_spec[:, BS:]], 0))
    grad_lat = dot3(latt_ref, jnp.concatenate(columns, 1))
    for k in range(KL):
        for h in range(HL):
            sg[pl.ds(k * HL + h, 2 * ROWS, stride=HL * KL), :] = grad_lat[
                h * 2 * ROWS : (h + 1) * 2 * ROWS, k * BS : (k + 1) * BS
            ]
    send_row(sg, rg, CHUNK, 3, False)

    spec_scale = 1.0 / math.sqrt(H * K)
    ln_scale = 1.0 / math.sqrt(H * W)
    for layer, (left_ref, right_ref) in enumerate(((spec_ref, gpre_ref), (hid_ref, gtwo_ref))):
        product = jnp.zeros((2 * BS, 2 * BS), F32)
        for k in range(KL):
            product = product + dot_c(left_ref[k], right_ref[k])
        product = product * spec_scale
        real = product[:BS, :BS] + product[BS:, BS:]
        imag = product[:BS, BS:] - product[BS:, :BS]
        for part, values in enumerate((real, imag)):
            for half in range(2):
                gw[pl.ds(layer * 4 + part * 2 + half, ROWS, stride=PIECE), :] = values[
                    half * ROWS : (half + 1) * ROWS
                ]
    gain_sum = (gain_sum[:, :BS] + gain_sum[:, BS:]) * ln_scale
    gw[pl.ds(PIECE - 1, ROWS, stride=PIECE), :] = jnp.concatenate(
        [
            one_sum[:, :BS] * spec_scale,
            one_sum[:, BS:] * spec_scale,
            two_sum[:, :BS] * spec_scale,
            two_sum[:, BS:] * spec_scale,
            gain_sum,
            shift_sum,
            jnp.zeros((ROWS - 6, BS), F32),
        ],
        0,
    )
    send_row(gw, rw, PIECE, 4, False)

    arrived(rg, 3)
    su[...] = jnp.zeros_like(su)
    grads = []
    for h in range(HL):
        grad_norm = dot3(lont_ref, rg[pl.ds(h, 2 * K, stride=HL), :]) * gain
        high, low = split(grad_norm)
        su[h : h + 1, :W] = (dot_t(ones_thin, high) + dot_t(ones_thin, low))[:1]
        high, low = split(grad_norm * normed_ref[h])
        su[HL + h : HL + h + 1, :W] = (dot_t(ones_thin, high) + dot_t(ones_thin, low))[:1]
        grads.append(grad_norm)
    send_chan(su, ru, 5)

    arrived(rw, 4)
    summed = rw[pl.ds(0, 8 * PIECE), :]
    for s in range(1, ROWS // 8):
        summed = summed + rw[pl.ds(s * 8 * PIECE, 8 * PIECE), :]
    fold[...] = summed
    summed = fold[pl.ds(0, PIECE), :]
    for s in range(1, 8):
        summed = summed + fold[pl.ds(s * PIECE, PIECE), :]
    piece[...] = summed
    send_row(piece, aw, PIECE, 6, True)

    arrived(ru, 5)
    total = ru[0]
    for c in range(1, CHANS):
        total = total + ru[c]
    wide = spread(total * (1.0 / C), W)
    for h in range(HL):
        one = wide[:, h * BS : (h + 1) * BS]
        two = wide[:, (HL + h) * BS : (HL + h + 1) * BS]
        inner = grads[h] - one - normed_ref[h] * two
        out_ref[0, h] = (cot_ref[0, h].astype(F32) + rstd_ref[h] * inner).astype(BF16)

    arrived(aw, 6)
    for layer, target in enumerate((gw1_ref, gw2_ref)):
        for part in range(2):
            for half in range(2):
                target[part, half * ROWS : (half + 1) * ROWS] = aw[
                    pl.ds(layer * 4 + part * 2 + half, ROWS, stride=PIECE), :
                ]
    extras = aw[pl.ds(PIECE - 1, 8, stride=PIECE), :]
    gb1_ref[...] = extras[0:2]
    gb2_ref[...] = extras[2:4]
    gg_ref[...] = extras[4:5]
    gs_ref[...] = extras[5:6]

    left(rt.at[pl.ds(0, CHANS - 1)], 0)
    left(ru.at[pl.ds(0, CHANS - 1)], 5)
    for which in (1, 2, 3):
        left(rc.at[pl.ds(0, LINES - CHUNK)], which)
    for which in (4, 6):
        left(rw.at[pl.ds(0, GLINES - PIECE)], which)


def on_device(
    inputs, cotangent, ln_gain, ln_shift, first_weight, first_bias, second_weight, second_bias
):
    lon = lon_table()
    lat = lat_table()
    tables = [jnp.asarray(halves(t)) for t in (lon, lon.T, lat, lat.T)]
    lines = pltpu.VMEM((LINES, BS), F32)
    glines = pltpu.VMEM((GLINES, BS), F32)
    stats = pltpu.VMEM((8, WPAD), F32)
    landed = pltpu.VMEM((CHANS, 8, WPAD), F32)
    grid = pltpu.VMEM((HL, W, BS), F32)
    wide = pltpu.VMEM((KL, H, 2 * BS), F32)
    narrow = pltpu.VMEM((KL, H, 2 * BS), BF16)
    in_vmem = pl.BlockSpec(memory_space=pltpu.VMEM)
    shape = jax.ShapeDtypeStruct
    outs = pl.pallas_call(
        kernel,
        out_shape=(
            shape((1, HL, W, BS), BF16),
            shape((2, BS, BS), F32),
            shape((2, BS), F32),
            shape((2, BS, BS), F32),
            shape((2, BS), F32),
            shape((1, BS), F32),
            shape((1, BS), F32),
        ),
        in_specs=[in_vmem] * 12,
        out_specs=(in_vmem,) * 7,
        scratch_shapes=[
            lines, lines, lines, lines, lines, lines,
            stats, landed, stats, landed, grid, grid,
            narrow, wide, narrow, wide, wide, narrow, narrow,
            glines, glines, pltpu.VMEM((8 * PIECE, BS), F32), pltpu.VMEM((PIECE, BS), F32), glines,
            pltpu.SemaphoreType.DMA((7,)),
            pltpu.SemaphoreType.DMA((7,)),
        ],
        compiler_params=pltpu.CompilerParams(
            collective_id=0, has_side_effects=True, vmem_limit_bytes=48 * 1024 * 1024
        ),
    )(
        inputs, cotangent, ln_gain.reshape(1, BS), ln_shift.reshape(1, BS),
        first_weight, first_bias, second_weight, second_bias, *tables,
    )
    return outs[:5] + (outs[5].reshape(BS), outs[6].reshape(BS))


def solution(mesh):
    placed = (
        P(None, "row", None, "chan"),
        P(None, "row", None, "chan"),
        P("chan"),
        P("chan"),
        P(None, "chan", None),
        P(None, "chan"),
        P(None, "chan", None),
        P(None, "chan"),
    )
    return jax.shard_map(
        on_device,
        mesh=mesh,
        in_specs=placed,
        out_specs=(
            P(None, "row", None, "chan"),
            P(None, "chan", None),
            P(None, "chan"),
            P(None, "chan", None),
            P(None, "chan"),
            P("chan"),
            P("chan"),
        ),
        check_vma=False,
    )
```

```python
import math

import jax
import jax.numpy as jnp
import ml_dtypes
import numpy as np
from jax import lax
from jax.experimental import pallas as pl
from jax.experimental.pallas import tpu as pltpu
from jax.sharding import PartitionSpec as P

H = 192
W = 448
K = 192
BS = 128
C = 1024
ZS, YS, CORES = 8, 4, 2
ROWS = ZS * YS * CORES
CHIPS = ZS * YS
XS = 4
CHANS = 2 * XS
HL = H // ROWS
KL = K // ROWS
CHUNK = 2 * HL
LINES = ROWS * CHUNK
PIECE = 9
GLINES = CHIPS * PIECE
WT = -(-W // BS)
SLINES = 2 * HL * WT

EPS = 1e-05
LAMBDA = 0.01
ROOT_TWO_PI = math.sqrt(2.0 / math.pi)
F32 = jnp.float32
BF16 = jnp.bfloat16
MESH = pl.DeviceIdType.MESH
COT, MIXED, GRAD = 0, KL, 2 * KL
STATS, SUMS, SWAP, SCATTER, GATHER, JOIN = (3 * KL + i for i in (0, 2, 4, 5, 6, 7))
SEMS = 3 * KL + 8


def halves(table):
    table = table.astype(np.float32)
    high = table.astype(ml_dtypes.bfloat16)
    low = (table - high.astype(np.float32)).astype(ml_dtypes.bfloat16)
    return np.stack([high, low])


def lon_table():
    kk = np.arange(KL).reshape(KL, 1, 1)
    owner = np.arange(ROWS).reshape(1, ROWS, 1)
    part = np.arange(2).reshape(1, 1, 2)
    number, part = np.broadcast_arrays(owner * KL + kk, part)
    number, part = number.reshape(-1, 1), part.reshape(-1, 1)
    phase = (number * np.arange(W)[None, :] % W) * (2.0 * math.pi / W)
    return np.where(part == 0, np.cos(phase), -np.sin(phase)) / math.sqrt(W)


def lat_table():
    q = np.arange(2).reshape(2, 1, 1, 1, 1)
    g = np.arange(H).reshape(1, H, 1, 1, 1)
    hh = np.arange(HL).reshape(1, 1, HL, 1, 1)
    s = np.arange(ROWS).reshape(1, 1, 1, ROWS, 1)
    p = np.arange(2).reshape(1, 1, 1, 1, 2)
    phase = (g * (s * HL + hh) % H) * (2.0 * math.pi / H)
    cosine, sine = np.cos(phase), np.sin(phase)
    table = np.where(q == p, cosine, np.where(q == 0, sine, -sine)) / math.sqrt(H)
    return table.reshape(2 * H, HL * ROWS * 2)


def lon_back_table():
    high, low = halves(lon_table())
    cut = lambda t: t.reshape(KL, 2 * ROWS, W).transpose(0, 2, 1)
    return np.concatenate([cut(high), cut(low), cut(high)], 2)


def dot(a, b):
    return lax.dot_general(a, b, (((1,), (0,)), ((), ())), preferred_element_type=F32)


def dot_t(a, b):
    return lax.dot_general(a, b, (((1,), (1,)), ((), ())), preferred_element_type=F32)


def dot_c(a, b):
    return lax.dot_general(a, b, (((0,), (0,)), ((), ())), preferred_element_type=F32)


def split(values):
    high = values.astype(BF16)
    return high, (values - high.astype(F32)).astype(BF16)


def dot3(table_high, table_low, values):
    high, low = split(values)
    return dot(table_high, high) + (dot(table_low, high) + dot(table_high, low))


def gelu_parts(values):
    square = values * values
    tangent = jnp.tanh(ROOT_TWO_PI * (values + 0.044715 * (square * values)))
    plus = 0.5 * (1.0 + tangent)
    slope = plus + 0.5 * values * (1.0 - tangent * tangent) * (
        ROOT_TWO_PI * (1.0 + 3.0 * 0.044715 * square)
    )
    return values * plus, slope


def block_matrix(weight):
    real, imag = weight[0], weight[1]
    return jnp.concatenate(
        [jnp.concatenate([real, imag], 1), jnp.concatenate([-imag, real], 1)], 0
    )


def diagonal(rows):
    return (
        lax.broadcasted_iota(jnp.int32, (rows, BS), 0)
        == lax.broadcasted_iota(jnp.int32, (rows, BS), 1)
    )


def pack(values):
    lines = []
    for t in range(WT):
        block = values[t * BS : min((t + 1) * BS, W)]
        lines.append(jnp.sum(jnp.where(diagonal(block.shape[0]), block, 0.0), 0, keepdims=True))
    return jnp.concatenate(lines, 0)


def spread(turned, line):
    blocks = []
    for t in range(WT):
        column = turned[: min(BS, W - t * BS), line + t : line + t + 1]
        blocks.append(jnp.broadcast_to(column, (column.shape[0], BS)))
    return jnp.concatenate(blocks, 0)


def kernel(*refs):
    sources, refs = refs[:12], refs[12:]
    held, refs = refs[-12:], refs[:-12]
    on_chip(sources, held, *held, *refs)


def on_chip(
    sources, held,
    cot_ref, lon_ref, x_ref, gain_ref, shift_ref, w1_ref, b1_ref, w2_ref, b2_ref,
    lat_ref, latt_ref, lont_ref,
    out_hbm, gw1_hbm, gb1_hbm, gw2_hbm, gb2_hbm, gg_hbm, gs_hbm,
    sc, rc, sx, rx, sg, rg, st, rt, su, ru, normed_ref, rstd_ref, grad_ref,
    dw_ref, gw, gx, hw, rw, fold, piece, aw,
    send_sem, recv_sem, load_sem, store_sem,
    out_ref, gw1_ref, gb1_ref, gw2_ref, gb2_ref, gg_ref, gs_ref,
):
    chan = lax.axis_index("chan")
    row = lax.axis_index("row")
    z, y, core = row // (YS * CORES), row // CORES % YS, row % CORES
    chip = row // CORES
    along_x = chan % XS
    chan_base = chan - along_x
    opposite = lax.rem(chan + XS, CHANS)
    twin = row + 1 - 2 * core

    def peer(i):
        other_z = lax.rem(z + i % ZS, ZS)
        other_y = lax.rem(y + i // (ZS * CORES), YS)
        other_core = lax.rem(core + i // ZS, CORES)
        return (other_z * YS + other_y) * CORES + other_core

    def peer_chip(i):
        return lax.rem(z + i % ZS, ZS) * YS + lax.rem(y + i // ZS, YS)

    def peer_x(i):
        return chan_base + lax.rem(along_x + i, XS)

    barrier = pltpu.get_barrier_semaphore()

    def greet(name, other):
        pl.semaphore_signal(barrier, inc=1, device_id={name: other}, device_id_type=MESH)

    def greet_row(i, carry):
        greet("row", peer(i))
        return carry

    lax.fori_loop(1, ROWS, greet_row, 0)
    for i in range(1, XS):
        greet("chan", peer_x(i))
    greet("chan", opposite)

    loads = [
        pltpu.make_async_copy(source, target, load_sem.at[i])
        for i, (source, target) in enumerate(zip(sources, held))
    ]
    for load in loads:
        load.start()

    def remote(source, target, which, name, other):
        return pltpu.make_async_remote_copy(
            src_ref=source,
            dst_ref=target,
            send_sem=send_sem.at[which],
            recv_sem=recv_sem.at[which],
            device_id={name: other},
            device_id_type=MESH,
        )

    def arrived(target, which):
        pltpu.make_async_copy(target, target, recv_sem.at[which]).wait()

    def left(target, which):
        pltpu.make_async_copy(target, target, send_sem.at[which]).wait()

    own = pl.ds(row * CHUNK, CHUNK)
    own_piece = pl.ds(chip * PIECE, PIECE)

    def send_chunks(source, target, k, which):
        def one(i, carry):
            other = peer(i)
            block = source.at[k, pl.ds(other * CHUNK, CHUNK)]
            remote(block, target.at[k, own], which + k, "row", other).start()
            return carry

        lax.fori_loop(1, ROWS, one, 0)
        pltpu.make_async_copy(
            source.at[k, own], target.at[k, own], recv_sem.at[which + k]
        ).start()

    for load in loads[:3]:
        load.wait()

    ones = jnp.ones((BS, BS), F32).astype(BF16)
    for h in range(HL):
        block = x_ref[0, h]
        amount = dot(block, ones)
        centred = block.astype(F32) - amount * (1.0 / BS)
        high, low = split(centred * centred)
        st[0, pl.ds(h * WT, WT), :] = pack(amount)
        st[0, pl.ds((HL + h) * WT, WT), :] = pack(dot(high, ones) + dot(low, ones))

    cot_wide = jnp.concatenate([cot_ref[0, h] for h in range(HL)], 1)

    def transform(k, product):
        rows = pl.ds(k * 2 * ROWS, 2 * ROWS)
        return product(lon_ref[0, rows, :], lon_ref[1, rows, :])

    def lay(target, k, values):
        for h in range(HL):
            target[k, pl.ds(h, 2 * ROWS, stride=HL), :] = values[:, h * BS : (h + 1) * BS]

    def cot_lon(k):
        lay(sc, k, transform(k, lambda high, low: dot(high, cot_wide) + dot(low, cot_wide)))

    cot_lon(0)

    pl.semaphore_wait(barrier, ROWS - 1 + XS)

    for i in range(1, XS):
        remote(st.at[0], rt.at[along_x], STATS, "chan", peer_x(i)).start()
    send_chunks(sc, rc, 0, COT)
    cot_lon(1)
    cot_lon(2)

    arrived(rt.at[pl.ds(0, XS - 1)], STATS)
    mine = st[0]

    def part(i):
        return jnp.where(along_x == i, mine, rt[i])

    parts = [part(i) for i in range(XS)]
    half = SLINES // 2
    amount = parts[0][:half] + parts[1][:half] + parts[2][:half] + parts[3][:half]
    squares = parts[0][half:] + parts[1][half:] + parts[2][half:] + parts[3][half:]
    average = amount * (1.0 / (XS * BS))
    for i in range(XS):
        away = parts[i][:half] * (1.0 / BS) - average
        squares = squares + BS * (away * away)
    st[1] = jnp.concatenate([amount, squares], 0)
    remote(st.at[1], rt.at[XS], STATS + 1, "chan", opposite).start()

    send_chunks(sc, rc, 1, COT)

    arrived(rt.at[XS], STATS + 1)
    amount_two = rt[XS, pl.ds(0, half), :]
    mean = (amount + amount_two) * (1.0 / C)
    away = average - mean
    away_two = amount_two * (1.0 / (XS * BS)) - mean
    squares = squares + rt[XS, pl.ds(half, half), :] + (XS * BS) * (
        away * away + away_two * away_two
    )
    rstd = lax.rsqrt(squares * (1.0 / C) + EPS)

    turned = jnp.concatenate([mean, rstd], 0).T
    for h in range(HL):
        scale = spread(turned, half + h * WT)
        normed_ref[:, h * BS : (h + 1) * BS] = (
            x_ref[0, h].astype(F32) - spread(turned, h * WT)
        ) * scale
        rstd_ref[:, h * BS : (h + 1) * BS] = scale
    high, low = split(normed_ref[...])

    def mixed_lon(k):
        lay(sx, k, transform(k, lambda a, b: dot(a, high) + (dot(b, high) + dot(a, low))))

    mixed_lon(0)
    send_chunks(sx, rx, 0, MIXED)
    mixed_lon(1)
    send_chunks(sx, rx, 1, MIXED)
    send_chunks(sc, rc, 2, COT)
    mixed_lon(2)
    send_chunks(sx, rx, 2, MIXED)

    for load in loads[3:]:
        load.wait()
    one_matrix = block_matrix(w1_ref)
    two_matrix = block_matrix(w2_ref)
    one_bias = jnp.concatenate([b1_ref[0:1], b1_ref[1:2]], 1)
    two_bias = jnp.concatenate([b2_ref[0:1], b2_ref[1:2]], 1)
    gain = gain_ref[...]
    gain_two = jnp.concatenate([gain, gain], 1)
    shift_two = jnp.concatenate([shift_ref[...] * math.sqrt(H * W), jnp.zeros((1, BS), F32)], 1)
    first = jnp.where(row == 0, 1.0, 0.0).astype(F32)
    spec_scale = 1.0 / math.sqrt(H * K)
    ln_scale = 1.0 / math.sqrt(H * W)

    def gathered(landed, k):
        return jnp.concatenate(
            [landed[k, pl.ds(h, 2 * ROWS, stride=HL), :] for h in range(HL)], 0
        )

    def tokens(values):
        return jnp.concatenate([values[:H], values[H:]], 1)

    gain_sum = jnp.zeros((1, 2 * BS), F32)
    one_sum = jnp.zeros((1, 2 * BS), F32)
    two_sum = jnp.zeros((1, 2 * BS), F32)
    for k in range(KL):
        arrived(rc.at[k], COT + k)
        arrived(rx.at[k], MIXED + k)
        both = dot3(
            lat_ref[0], lat_ref[1], jnp.concatenate([gathered(rx, k), gathered(rc, k)], 1)
        )
        plain = tokens(both[:, :BS])
        mixed = plain * gain_two
        if k == 0:
            line = lax.broadcasted_iota(jnp.int32, (H, 2 * BS), 0)
            mixed = mixed + jnp.where(line == 0, shift_two * first, 0.0)
        rounded = mixed.astype(BF16)
        act, slope = gelu_parts(dot(rounded, one_matrix) + one_bias)
        hidden = act.astype(BF16)
        tangent = jnp.tanh((dot(hidden, two_matrix) + two_bias) * (1.0 / LAMBDA))
        cot_block = tokens(both[:, BS:]) * (2.0 - first if k == 0 else 2.0)
        grad_two = (cot_block * (tangent * tangent)).astype(BF16)
        grad_pre = (dot_t(grad_two, two_matrix) * slope).astype(BF16)
        grad_spec = dot_t(grad_pre, one_matrix)
        grad_lat = dot3(
            latt_ref[0], latt_ref[1],
            jnp.concatenate([grad_spec[:, :BS], grad_spec[:, BS:]], 0),
        )
        for h in range(HL):
            sg[k, pl.ds(h, 2 * ROWS, stride=HL), :] = grad_lat[h * 2 * ROWS : (h + 1) * 2 * ROWS]
        if k < KL - 1:
            send_chunks(sg, rg, k, GRAD)
        two_sum = two_sum + jnp.sum(grad_two.astype(F32), 0, keepdims=True)
        one_sum = one_sum + jnp.sum(grad_pre.astype(F32), 0, keepdims=True)
        gain_sum = gain_sum + jnp.sum(grad_spec * plain, 0, keepdims=True)
        if k == 0:
            shift_sum = grad_spec[0:1, :BS] * first
        for layer, (before, after) in enumerate(((rounded, grad_pre), (hidden, grad_two))):
            product = dot_c(before, after)
            dw_ref[layer] = product if k == 0 else dw_ref[layer] + product

    for layer in range(2):
        product = dw_ref[layer] * spec_scale
        real = product[:BS, :BS] + product[BS:, BS:]
        imag = product[:BS, BS:] - product[BS:, :BS]
        for part_index, values in enumerate((real, imag)):
            for c in range(CORES):
                for sub in range(2):
                    start = (c * 2 + sub) * CHIPS
                    gw[c, pl.ds(layer * 4 + part_index * 2 + sub, CHIPS, stride=PIECE), :] = (
                        values[start : start + CHIPS]
                    )
    gain_sum = (gain_sum[:, :BS] + gain_sum[:, BS:]) * ln_scale
    gw[0, pl.ds(PIECE - 1, CHIPS, stride=PIECE), :] = jnp.concatenate(
        [
            one_sum[:, :BS] * spec_scale,
            one_sum[:, BS:] * spec_scale,
            two_sum[:, :BS] * spec_scale,
            two_sum[:, BS:] * spec_scale,
            gain_sum,
            shift_sum,
            jnp.zeros((CHIPS - 6, BS), F32),
        ],
        0,
    )
    gw[1, pl.ds(PIECE - 1, CHIPS, stride=PIECE), :] = jnp.zeros((CHIPS, BS), F32)
    remote(gw.at[1 - core], gx, SWAP, "row", twin).start()
    arrived(gx, SWAP)
    hw[...] = gw[core] + gx[...]

    def scatter(i, carry):
        other = peer_chip(i)
        block = hw.at[pl.ds(other * PIECE, PIECE)]
        remote(block, rw.at[own_piece], SCATTER, "row", other * CORES + core).start()
        return carry

    lax.fori_loop(1, CHIPS, scatter, 0)
    pltpu.make_async_copy(hw.at[own_piece], rw.at[own_piece], recv_sem.at[SCATTER]).start()
    send_chunks(sg, rg, KL - 1, GRAD)

    def lon_back(k):
        values = jnp.concatenate(
            [rg[k, pl.ds(h, 2 * ROWS, stride=HL), :] for h in range(HL)], 1
        )
        high, low = split(values)
        return dot(lont_ref[k], jnp.concatenate([high, high, low], 0))

    arrived(rg.at[0], GRAD)
    grad_ref[...] = lon_back(0)
    arrived(rg.at[1], GRAD + 1)
    grad_ref[...] = grad_ref[...] + lon_back(1)

    arrived(rw, SCATTER)
    slab = 8 * PIECE
    summed = rw[pl.ds(0, slab), :]
    for s in range(1, CHIPS // 8):
        summed = summed + rw[pl.ds(s * slab, slab), :]
    fold[...] = summed
    summed = fold[pl.ds(0, PIECE), :]
    for s in range(1, 8):
        summed = summed + fold[pl.ds(s * PIECE, PIECE), :]
    piece[...] = summed

    def gather(i, carry):
        other = peer_chip(i)
        remote(piece, aw.at[core, own_piece], GATHER, "row", other * CORES + core).start()
        return carry

    lax.fori_loop(1, CHIPS, gather, 0)
    pltpu.make_async_copy(piece, aw.at[core, own_piece], recv_sem.at[GATHER]).start()

    arrived(rg.at[2], GRAD + 2)
    zeros = jnp.zeros((BS, BS), F32).astype(BF16)
    pair = jnp.concatenate(
        [jnp.concatenate([ones, zeros], 1), jnp.concatenate([zeros, ones], 1)], 0
    )
    gain_wide = jnp.concatenate([gain] * HL, 1)
    grad_ref[...] = (grad_ref[...] + lon_back(2)) * gain_wide
    for h in range(HL):
        grad_norm = grad_ref[:, h * BS : (h + 1) * BS]
        product = grad_norm * normed_ref[:, h * BS : (h + 1) * BS]
        sums = dot(jnp.concatenate([grad_norm.astype(BF16), product.astype(BF16)], 1), pair)
        su[0, pl.ds(h * WT, WT), :] = pack(sums[:, :BS])
        su[0, pl.ds((HL + h) * WT, WT), :] = pack(sums[:, BS:])
    for i in range(1, XS):
        remote(su.at[0], ru.at[along_x], SUMS, "chan", peer_x(i)).start()
    arrived(ru.at[pl.ds(0, XS - 1)], SUMS)
    mine = su[0]
    total = jnp.where(along_x == 0, mine, ru[0])
    for i in range(1, XS):
        total = total + jnp.where(along_x == i, mine, ru[i])
    su[1] = total
    remote(su.at[1], ru.at[XS], SUMS + 1, "chan", opposite).start()

    arrived(aw.at[core], GATHER)
    remote(aw.at[core], aw.at[core], JOIN, "row", twin).start()

    arrived(ru.at[XS], SUMS + 1)
    turned = ((total + ru[XS]) * (1.0 / C)).T
    stores = []
    for h in range(HL):
        lanes = slice(h * BS, (h + 1) * BS)
        inner = grad_ref[:, lanes] - spread(turned, h * WT) - normed_ref[:, lanes] * spread(
            turned, half + h * WT
        )
        out_ref[0, h] = (cot_ref[0, h].astype(F32) + rstd_ref[:, lanes] * inner).astype(BF16)
        stores.append(pltpu.make_async_copy(out_ref.at[0, h], out_hbm.at[0, h], store_sem.at[h]))
        stores[-1].start()

    arrived(aw.at[1 - core], JOIN)
    for layer, target in enumerate((gw1_ref, gw2_ref)):
        for part_index in range(2):
            for c in range(CORES):
                for sub in range(2):
                    start = (c * 2 + sub) * CHIPS
                    target[part_index, start : start + CHIPS] = aw[
                        c, pl.ds(layer * 4 + part_index * 2 + sub, CHIPS, stride=PIECE), :
                    ]
    extras = aw[0, pl.ds(PIECE - 1, 8, stride=PIECE), :]
    gb1_ref[...] = extras[0:2]
    gb2_ref[...] = extras[2:4]
    gg_ref[...] = extras[4:5]
    gs_ref[...] = extras[5:6]
    for i, (source, target) in enumerate(
        (
            (gw1_ref, gw1_hbm), (gb1_ref, gb1_hbm), (gw2_ref, gw2_hbm),
            (gb2_ref, gb2_hbm), (gg_ref, gg_hbm), (gs_ref, gs_hbm),
        )
    ):
        stores.append(pltpu.make_async_copy(source, target, store_sem.at[HL + i]))
        stores[-1].start()

    for which in (STATS, SUMS):
        left(rt.at[pl.ds(0, XS - 1)], which)
        left(rt.at[XS], which + 1)
    for k in range(KL):
        for which in (COT, MIXED, GRAD):
            left(rc.at[0, pl.ds(0, LINES - CHUNK)], which + k)
    for which in (SWAP, JOIN):
        left(hw, which)
    for which in (SCATTER, GATHER):
        left(hw.at[pl.ds(0, GLINES - PIECE)], which)
    for store in stores:
        store.wait()


def hand_out(*refs):
    given, wanted, held = refs[:7], refs[7:14], refs[14:21]
    in_sem, out_sem = refs[21:]
    brought = [pltpu.make_async_copy(given[i], held[i], in_sem.at[i]) for i in range(7)]
    taken = [pltpu.make_async_copy(held[i], wanted[i], out_sem.at[i]) for i in range(7)]
    for copy in brought:
        copy.start()
    for first, second in zip(brought, taken):
        first.wait()
        second.start()
    for copy in taken:
        copy.wait()


def on_device(
    inputs, cotangent, ln_gain, ln_shift, first_weight, first_bias, second_weight, second_bias
):
    lat = lat_table()
    lon, lat, latt, lont = (
        jnp.asarray(t)
        for t in (halves(lon_table()), halves(lat), halves(lat.T), lon_back_table())
    )
    sources = (
        cotangent, lon, inputs, ln_gain.reshape(1, BS), ln_shift.reshape(1, BS),
        first_weight, first_bias, second_weight, second_bias, lat, latt, lont,
    )
    lines = pltpu.VMEM((KL, LINES, BS), F32)
    glines = pltpu.VMEM((GLINES, BS), F32)
    stats = pltpu.VMEM((2, SLINES, BS), F32)
    landed = pltpu.VMEM((XS + 1, SLINES, BS), F32)
    grid = pltpu.VMEM((W, HL * BS), F32)
    shape = jax.ShapeDtypeStruct
    results = (
        shape((1, HL, W, BS), BF16),
        shape((2, BS, BS), F32),
        shape((2, BS), F32),
        shape((2, BS, BS), F32),
        shape((2, BS), F32),
        shape((1, BS), F32),
        shape((1, BS), F32),
    )
    in_hbm = pl.BlockSpec(memory_space=pltpu.HBM)
    outs = pl.pallas_call(
        kernel,
        out_shape=results,
        in_specs=[in_hbm] * 12,
        out_specs=(in_hbm,) * 7,
        scratch_shapes=[
            lines, lines, lines, lines, lines, lines,
            stats, landed, stats, landed, grid, grid, grid,
            pltpu.VMEM((2, 2 * BS, 2 * BS), F32),
            pltpu.VMEM((CORES, GLINES, BS), F32), glines, glines, glines,
            pltpu.VMEM((8 * PIECE, BS), F32), pltpu.VMEM((PIECE, BS), F32),
            pltpu.VMEM((CORES, GLINES, BS), F32),
            pltpu.SemaphoreType.DMA((SEMS,)),
            pltpu.SemaphoreType.DMA((SEMS,)),
            pltpu.SemaphoreType.DMA((12,)),
            pltpu.SemaphoreType.DMA((HL + 6,)),
        ]
        + [pltpu.VMEM(r.shape, r.dtype) for r in results]
        + [pltpu.VMEM(source.shape, source.dtype) for source in sources],
        compiler_params=pltpu.CompilerParams(
            collective_id=0, has_side_effects=True, vmem_limit_bytes=64 * 1024 * 1024
        ),
    )(*sources)
    outs = pl.pallas_call(
        hand_out,
        out_shape=results,
        in_specs=[in_hbm] * 7,
        out_specs=(in_hbm,) * 7,
        scratch_shapes=[pltpu.VMEM(r.shape, r.dtype) for r in results]
        + [pltpu.SemaphoreType.DMA((7,))] * 2,
        compiler_params=pltpu.CompilerParams(vmem_limit_bytes=64 * 1024 * 1024),
    )(*outs)
    return tuple(outs[:5]) + (outs[5].reshape(BS), outs[6].reshape(BS))


def solution(mesh):
    placed = (
        P(None, "row", None, "chan"),
        P(None, "row", None, "chan"),
        P("chan"),
        P("chan"),
        P(None, "chan", None),
        P(None, "chan"),
        P(None, "chan", None),
        P(None, "chan"),
    )
    return jax.shard_map(
        on_device,
        mesh=mesh,
        in_specs=placed,
        out_specs=(
            P(None, "row", None, "chan"),
            P(None, "chan", None),
            P(None, "chan"),
            P(None, "chan", None),
            P(None, "chan"),
            P("chan"),
            P("chan"),
        ),
        check_vma=False,
    )
```

```python
import math

import jax
import jax.numpy as jnp
import ml_dtypes
import numpy as np
from jax import lax
from jax.experimental import pallas as pl
from jax.experimental.pallas import tpu as pltpu
from jax.sharding import PartitionSpec as P

H = 192
W = 448
K = 192
BS = 128
C = 1024
ZS, YS, CORES = 8, 4, 2
ROWS = ZS * YS * CORES
CHIPS = ZS * YS
XS = 4
CHANS = 2 * XS
HL = H // ROWS
KL = K // ROWS
CHUNK = 2 * HL
LINES = ROWS * CHUNK
PIECE = 9
GLINES = CHIPS * PIECE
WT = -(-W // BS)
SLINES = 2 * HL * WT

EPS = 1e-05
LAMBDA = 0.01
ROOT_TWO_PI = math.sqrt(2.0 / math.pi)
F32 = jnp.float32
BF16 = jnp.bfloat16
MESH = pl.DeviceIdType.MESH
COT, MIXED, GRAD = 0, KL, 2 * KL
STATS, SUMS, SWAP, SCATTER, GATHER, JOIN = (3 * KL + i for i in (0, 2, 4, 5, 6, 7))
SEMS = 3 * KL + 8


def halves(table):
    table = table.astype(np.float32)
    high = table.astype(ml_dtypes.bfloat16)
    low = (table - high.astype(np.float32)).astype(ml_dtypes.bfloat16)
    return np.stack([high, low])


def lon_table():
    kk = np.arange(KL).reshape(KL, 1, 1)
    owner = np.arange(ROWS).reshape(1, ROWS, 1)
    part = np.arange(2).reshape(1, 1, 2)
    number, part = np.broadcast_arrays(owner * KL + kk, part)
    number, part = number.reshape(-1, 1), part.reshape(-1, 1)
    phase = (number * np.arange(W)[None, :] % W) * (2.0 * math.pi / W)
    return np.where(part == 0, np.cos(phase), -np.sin(phase)) / math.sqrt(W)


def lat_table():
    q = np.arange(2).reshape(2, 1, 1, 1, 1)
    g = np.arange(H).reshape(1, H, 1, 1, 1)
    hh = np.arange(HL).reshape(1, 1, HL, 1, 1)
    s = np.arange(ROWS).reshape(1, 1, 1, ROWS, 1)
    p = np.arange(2).reshape(1, 1, 1, 1, 2)
    phase = (g * (s * HL + hh) % H) * (2.0 * math.pi / H)
    cosine, sine = np.cos(phase), np.sin(phase)
    table = np.where(q == p, cosine, np.where(q == 0, sine, -sine)) / math.sqrt(H)
    return table.reshape(2 * H, HL * ROWS * 2)


def lon_back_table():
    high, low = halves(lon_table())
    cut = lambda t: t.reshape(KL, 2 * ROWS, W).transpose(0, 2, 1)
    return np.concatenate([cut(high), cut(low), cut(high)], 2)


def dot(a, b):
    return lax.dot_general(a, b, (((1,), (0,)), ((), ())), preferred_element_type=F32)


def dot_t(a, b):
    return lax.dot_general(a, b, (((1,), (1,)), ((), ())), preferred_element_type=F32)


def dot_c(a, b):
    return lax.dot_general(a, b, (((0,), (0,)), ((), ())), preferred_element_type=F32)


def split(values):
    high = values.astype(BF16)
    return high, (values - high.astype(F32)).astype(BF16)


def dot3(table_high, table_low, values):
    high, low = split(values)
    return dot(table_high, high) + (dot(table_low, high) + dot(table_high, low))


def gelu_parts(values):
    square = values * values
    tangent = jnp.tanh(ROOT_TWO_PI * (values + 0.044715 * (square * values)))
    plus = 0.5 * (1.0 + tangent)
    slope = plus + 0.5 * values * (1.0 - tangent * tangent) * (
        ROOT_TWO_PI * (1.0 + 3.0 * 0.044715 * square)
    )
    return values * plus, slope


def block_matrix(weight):
    real, imag = weight[0], weight[1]
    return jnp.concatenate(
        [jnp.concatenate([real, imag], 1), jnp.concatenate([-imag, real], 1)], 0
    )


def diagonal(rows):
    return (
        lax.broadcasted_iota(jnp.int32, (rows, BS), 0)
        == lax.broadcasted_iota(jnp.int32, (rows, BS), 1)
    )


def pack(values):
    lines = []
    for t in range(WT):
        block = values[t * BS : min((t + 1) * BS, W)]
        lines.append(jnp.sum(jnp.where(diagonal(block.shape[0]), block, 0.0), 0, keepdims=True))
    return jnp.concatenate(lines, 0)


def spread(turned, line):
    blocks = []
    for t in range(WT):
        column = turned[: min(BS, W - t * BS), line + t : line + t + 1]
        blocks.append(jnp.broadcast_to(column, (column.shape[0], BS)))
    return jnp.concatenate(blocks, 0)


def kernel(*refs):
    sources, refs = refs[:12], refs[12:]
    held, refs = refs[-12:], refs[:-12]
    on_chip(sources, held, *held, *refs)


def on_chip(
    sources, held,
    cot_ref, lon_ref, x_ref, gain_ref, shift_ref, w1_ref, b1_ref, w2_ref, b2_ref,
    lat_ref, latt_ref, lont_ref,
    out_ref, gw1_ref, gb1_ref, gw2_ref, gb2_ref, gg_ref, gs_ref,
    sc, rc, sx, rx, sg, rg, st, rt, su, ru, normed_ref, rstd_ref, grad_ref,
    dw_ref, gw, gx, hw, rw, fold, piece, aw,
    send_sem, recv_sem, load_sem,
):
    chan = lax.axis_index("chan")
    row = lax.axis_index("row")
    z, y, core = row // (YS * CORES), row // CORES % YS, row % CORES
    chip = row // CORES
    along_x = chan % XS
    chan_base = chan - along_x
    opposite = lax.rem(chan + XS, CHANS)
    twin = row + 1 - 2 * core

    ahead = [lax.rem(z + i, ZS) for i in range(ZS)]
    row_of = [a * (YS * CORES) for a in ahead]
    chip_of = [a * YS for a in ahead]

    def each_row(act, steps=tuple(range(ZS))):
        def level(i, carry):
            base = lax.rem(y + i // CORES, YS) * CORES + lax.rem(core + i, CORES)
            for step in steps:
                act(row_of[step] + base)
            return carry

        for step in steps:
            if step:
                act(row_of[step] + y * CORES + core)
        lax.fori_loop(1, YS * CORES, level, 0)

    def each_chip(act):
        def level(i, carry):
            base = lax.rem(y + i, YS)
            for offset in chip_of:
                act(offset + base)
            return carry

        for offset in chip_of[1:]:
            act(offset + y)
        lax.fori_loop(1, YS, level, 0)

    def peer_x(i):
        return chan_base + lax.rem(along_x + i, XS)

    loads = [
        pltpu.make_async_copy(source, target, load_sem.at[i])
        for i, (source, target) in enumerate(zip(sources, held))
    ]
    for load in loads[:3]:
        load.start()
    barrier = pltpu.get_barrier_semaphore()

    def greet(name, other):
        pl.semaphore_signal(barrier, inc=1, device_id={name: other}, device_id_type=MESH)

    for i in range(1, CHANS):
        greet("chan", lax.rem(chan + i, CHANS))
    each_row(lambda other: greet("row", other), (4, 3, 5, 2, 6, 1, 7, 0))

    def remote(source, target, which, name, other):
        return pltpu.make_async_remote_copy(
            src_ref=source,
            dst_ref=target,
            send_sem=send_sem.at[which],
            recv_sem=recv_sem.at[which],
            device_id={name: other},
            device_id_type=MESH,
        )

    def arrived(target, which):
        pltpu.make_async_copy(target, target, recv_sem.at[which]).wait()

    def left(target, which):
        pltpu.make_async_copy(target, target, send_sem.at[which]).wait()

    own = pl.ds(row * CHUNK, CHUNK)
    own_piece = pl.ds(chip * PIECE, PIECE)

    def send_chunks(source, target, k, which):
        def one(other):
            block = source.at[k, pl.ds(other * CHUNK, CHUNK)]
            remote(block, target.at[k, own], which + k, "row", other).start()

        each_row(one)
        pltpu.make_async_copy(
            source.at[k, own], target.at[k, own], recv_sem.at[which + k]
        ).start()

    for load in loads[:2]:
        load.wait()
    cot_wide = jnp.concatenate([cot_ref[0, h] for h in range(HL)], 1)

    def transform(k, product):
        rows = pl.ds(k * 2 * ROWS, 2 * ROWS)
        return product(lon_ref[0, rows, :], lon_ref[1, rows, :])

    def lay(target, k, values):
        for h in range(HL):
            target[k, pl.ds(h, 2 * ROWS, stride=HL), :] = values[:, h * BS : (h + 1) * BS]

    def cot_lon(k):
        lay(sc, k, transform(k, lambda high, low: dot(high, cot_wide) + dot(low, cot_wide)))

    cot_lon(0)

    loads[2].wait()
    ones = jnp.ones((BS, BS), F32).astype(BF16)
    for h in range(HL):
        block = x_ref[0, h]
        amount = dot(block, ones)
        centred = block.astype(F32) - amount * (1.0 / BS)
        high, low = split(centred * centred)
        st[0, pl.ds(h * WT, WT), :] = pack(amount)
        st[0, pl.ds((HL + h) * WT, WT), :] = pack(dot(high, ones) + dot(low, ones))
    pl.semaphore_wait(barrier, ROWS - 1 + CHANS - 1)

    for i in range(1, XS):
        remote(st.at[0], rt.at[along_x], STATS, "chan", peer_x(i)).start()
    send_chunks(sc, rc, 0, COT)
    cot_lon(1)
    cot_lon(2)

    arrived(rt.at[pl.ds(0, XS - 1)], STATS)
    mine = st[0]

    def part(i):
        return jnp.where(along_x == i, mine, rt[i])

    parts = [part(i) for i in range(XS)]
    half = SLINES // 2
    amount = parts[0][:half] + parts[1][:half] + parts[2][:half] + parts[3][:half]
    squares = parts[0][half:] + parts[1][half:] + parts[2][half:] + parts[3][half:]
    average = amount * (1.0 / (XS * BS))
    for i in range(XS):
        away = parts[i][:half] * (1.0 / BS) - average
        squares = squares + BS * (away * away)
    st[1] = jnp.concatenate([amount, squares], 0)
    remote(st.at[1], rt.at[XS], STATS + 1, "chan", opposite).start()

    send_chunks(sc, rc, 1, COT)
    send_chunks(sc, rc, 2, COT)
    for load in loads[3:]:
        load.start()

    arrived(rt.at[XS], STATS + 1)
    amount_two = rt[XS, pl.ds(0, half), :]
    mean = (amount + amount_two) * (1.0 / C)
    away = average - mean
    away_two = amount_two * (1.0 / (XS * BS)) - mean
    squares = squares + rt[XS, pl.ds(half, half), :] + (XS * BS) * (
        away * away + away_two * away_two
    )
    rstd = lax.rsqrt(squares * (1.0 / C) + EPS)

    turned = jnp.concatenate([mean, rstd], 0).T
    for h in range(HL):
        scale = spread(turned, half + h * WT)
        normed_ref[:, h * BS : (h + 1) * BS] = (
            x_ref[0, h].astype(F32) - spread(turned, h * WT)
        ) * scale
        rstd_ref[:, h * BS : (h + 1) * BS] = scale
    high, low = split(normed_ref[...])

    def mixed_lon(k):
        lay(sx, k, transform(k, lambda a, b: dot(a, high) + (dot(b, high) + dot(a, low))))

    mixed_lon(0)
    send_chunks(sx, rx, 0, MIXED)
    mixed_lon(1)
    send_chunks(sx, rx, 1, MIXED)
    mixed_lon(2)
    send_chunks(sx, rx, 2, MIXED)

    for load in loads[3:]:
        load.wait()
    one_matrix = block_matrix(w1_ref)
    two_matrix = block_matrix(w2_ref)
    one_bias = jnp.concatenate([b1_ref[0:1], b1_ref[1:2]], 1)
    two_bias = jnp.concatenate([b2_ref[0:1], b2_ref[1:2]], 1)
    gain = gain_ref[...]
    gain_two = jnp.concatenate([gain, gain], 1)
    shift_two = jnp.concatenate([shift_ref[...] * math.sqrt(H * W), jnp.zeros((1, BS), F32)], 1)
    first = jnp.where(row == 0, 1.0, 0.0).astype(F32)
    spec_scale = 1.0 / math.sqrt(H * K)
    ln_scale = 1.0 / math.sqrt(H * W)

    def gathered(landed, k):
        return jnp.concatenate(
            [landed[k, pl.ds(h, 2 * ROWS, stride=HL), :] for h in range(HL)], 0
        )

    def tokens(values):
        return jnp.concatenate([values[:H], values[H:]], 1)

    gain_sum = jnp.zeros((1, 2 * BS), F32)
    one_sum = jnp.zeros((1, 2 * BS), F32)
    two_sum = jnp.zeros((1, 2 * BS), F32)
    for k in range(KL):
        arrived(rc.at[k], COT + k)
        arrived(rx.at[k], MIXED + k)
        both = dot3(
            lat_ref[0], lat_ref[1], jnp.concatenate([gathered(rx, k), gathered(rc, k)], 1)
        )
        plain = tokens(both[:, :BS])
        mixed = plain * gain_two
        if k == 0:
            line = lax.broadcasted_iota(jnp.int32, (H, 2 * BS), 0)
            mixed = mixed + jnp.where(line == 0, shift_two * first, 0.0)
        rounded = mixed.astype(BF16)
        act, slope = gelu_parts(dot(rounded, one_matrix) + one_bias)
        hidden = act.astype(BF16)
        tangent = jnp.tanh((dot(hidden, two_matrix) + two_bias) * (1.0 / LAMBDA))
        cot_block = tokens(both[:, BS:]) * (2.0 - first if k == 0 else 2.0)
        grad_two = (cot_block * (tangent * tangent)).astype(BF16)
        grad_pre = (dot_t(grad_two, two_matrix) * slope).astype(BF16)
        grad_spec = dot_t(grad_pre, one_matrix)
        grad_lat = dot3(
            latt_ref[0], latt_ref[1],
            jnp.concatenate([grad_spec[:, :BS], grad_spec[:, BS:]], 0),
        )
        for h in range(HL):
            sg[k, pl.ds(h, 2 * ROWS, stride=HL), :] = grad_lat[h * 2 * ROWS : (h + 1) * 2 * ROWS]
        if k < KL - 1:
            send_chunks(sg, rg, k, GRAD)
        two_sum = two_sum + jnp.sum(grad_two.astype(F32), 0, keepdims=True)
        one_sum = one_sum + jnp.sum(grad_pre.astype(F32), 0, keepdims=True)
        gain_sum = gain_sum + jnp.sum(grad_spec * plain, 0, keepdims=True)
        if k == 0:
            shift_sum = grad_spec[0:1, :BS] * first
        for layer, (before, after) in enumerate(((rounded, grad_pre), (hidden, grad_two))):
            product = dot_c(before, after)
            dw_ref[layer] = product if k == 0 else dw_ref[layer] + product

    for layer in range(2):
        product = dw_ref[layer] * spec_scale
        real = product[:BS, :BS] + product[BS:, BS:]
        imag = product[:BS, BS:] - product[BS:, :BS]
        for part_index, values in enumerate((real, imag)):
            for c in range(CORES):
                for sub in range(2):
                    start = (c * 2 + sub) * CHIPS
                    gw[c, pl.ds(layer * 4 + part_index * 2 + sub, CHIPS, stride=PIECE), :] = (
                        values[start : start + CHIPS]
                    )
    gain_sum = (gain_sum[:, :BS] + gain_sum[:, BS:]) * ln_scale
    gw[0, pl.ds(PIECE - 1, CHIPS, stride=PIECE), :] = jnp.concatenate(
        [
            one_sum[:, :BS] * spec_scale,
            one_sum[:, BS:] * spec_scale,
            two_sum[:, :BS] * spec_scale,
            two_sum[:, BS:] * spec_scale,
            gain_sum,
            shift_sum,
            jnp.zeros((CHIPS - 6, BS), F32),
        ],
        0,
    )
    gw[1, pl.ds(PIECE - 1, CHIPS, stride=PIECE), :] = jnp.zeros((CHIPS, BS), F32)
    remote(gw.at[1 - core], gx, SWAP, "row", twin).start()
    arrived(gx, SWAP)
    hw[...] = gw[core] + gx[...]

    def scatter(other):
        block = hw.at[pl.ds(other * PIECE, PIECE)]
        remote(block, rw.at[own_piece], SCATTER, "row", other * CORES + core).start()

    each_chip(scatter)
    pltpu.make_async_copy(hw.at[own_piece], rw.at[own_piece], recv_sem.at[SCATTER]).start()
    send_chunks(sg, rg, KL - 1, GRAD)

    def lon_back(k):
        values = jnp.concatenate(
            [rg[k, pl.ds(h, 2 * ROWS, stride=HL), :] for h in range(HL)], 1
        )
        high, low = split(values)
        return dot(lont_ref[k], jnp.concatenate([high, high, low], 0))

    arrived(rg.at[0], GRAD)
    grad_ref[...] = lon_back(0)
    arrived(rg.at[1], GRAD + 1)
    grad_ref[...] = grad_ref[...] + lon_back(1)

    arrived(rw, SCATTER)
    slab = 8 * PIECE
    summed = rw[pl.ds(0, slab), :]
    for s in range(1, CHIPS // 8):
        summed = summed + rw[pl.ds(s * slab, slab), :]
    fold[...] = summed
    summed = fold[pl.ds(0, PIECE), :]
    for s in range(1, 8):
        summed = summed + fold[pl.ds(s * PIECE, PIECE), :]
    piece[...] = summed

    def gather(other):
        remote(piece, aw.at[core, own_piece], GATHER, "row", other * CORES + core).start()

    each_chip(gather)
    pltpu.make_async_copy(piece, aw.at[core, own_piece], recv_sem.at[GATHER]).start()

    arrived(rg.at[2], GRAD + 2)
    zeros = jnp.zeros((BS, BS), F32).astype(BF16)
    pair = jnp.concatenate(
        [jnp.concatenate([ones, zeros], 1), jnp.concatenate([zeros, ones], 1)], 0
    )
    gain_wide = jnp.concatenate([gain] * HL, 1)
    grad_ref[...] = (grad_ref[...] + lon_back(2)) * gain_wide
    for h in range(HL):
        grad_norm = grad_ref[:, h * BS : (h + 1) * BS]
        product = grad_norm * normed_ref[:, h * BS : (h + 1) * BS]
        sums = dot(jnp.concatenate([grad_norm.astype(BF16), product.astype(BF16)], 1), pair)
        su[pl.ds(h * WT, WT), :] = pack(sums[:, :BS])
        su[pl.ds((HL + h) * WT, WT), :] = pack(sums[:, BS:])
    for i in range(1, CHANS):
        remote(su, ru.at[chan], SUMS, "chan", lax.rem(chan + i, CHANS)).start()
    pltpu.make_async_copy(su, ru.at[chan], recv_sem.at[SUMS]).start()

    arrived(aw.at[core], GATHER)
    remote(aw.at[core], aw.at[core], JOIN, "row", twin).start()

    arrived(ru, SUMS)
    total = ru[0]
    for i in range(1, CHANS):
        total = total + ru[i]
    turned = (total * (1.0 / C)).T
    for h in range(HL):
        lanes = slice(h * BS, (h + 1) * BS)
        inner = grad_ref[:, lanes] - spread(turned, h * WT) - normed_ref[:, lanes] * spread(
            turned, half + h * WT
        )
        out_ref[0, h] = (cot_ref[0, h].astype(F32) + rstd_ref[:, lanes] * inner).astype(BF16)

    arrived(aw.at[1 - core], JOIN)
    for layer, target in enumerate((gw1_ref, gw2_ref)):
        for part_index in range(2):
            for c in range(CORES):
                for sub in range(2):
                    start = (c * 2 + sub) * CHIPS
                    target[part_index, start : start + CHIPS] = aw[
                        c, pl.ds(layer * 4 + part_index * 2 + sub, CHIPS, stride=PIECE), :
                    ]
    extras = aw[0, pl.ds(PIECE - 1, 8, stride=PIECE), :]
    gb1_ref[...] = extras[0:2]
    gb2_ref[...] = extras[2:4]
    gg_ref[...] = extras[4:5]
    gs_ref[...] = extras[5:6]

    left(rt.at[pl.ds(0, XS - 1)], STATS)
    left(rt.at[XS], STATS + 1)
    left(ru.at[pl.ds(0, CHANS - 1)], SUMS)
    for k in range(KL):
        for which in (COT, MIXED, GRAD):
            left(rc.at[0, pl.ds(0, LINES - CHUNK)], which + k)
    for which in (SWAP, JOIN):
        left(hw, which)
    for which in (SCATTER, GATHER):
        left(hw.at[pl.ds(0, GLINES - PIECE)], which)


def hand_out(*refs):
    sem = refs[14]
    copies = [pltpu.make_async_copy(refs[i], refs[7 + i], sem.at[i]) for i in range(7)]
    for copy in copies:
        copy.start()
    for copy in copies:
        copy.wait()


def on_device(
    inputs, cotangent, ln_gain, ln_shift, first_weight, first_bias, second_weight, second_bias
):
    lat = lat_table()
    lon, lat, latt, lont = (
        jnp.asarray(t)
        for t in (halves(lon_table()), halves(lat), halves(lat.T), lon_back_table())
    )
    sources = (
        cotangent, lon, inputs, ln_gain.reshape(1, BS), ln_shift.reshape(1, BS),
        first_weight, first_bias, second_weight, second_bias, lat, latt, lont,
    )
    lines = pltpu.VMEM((KL, LINES, BS), F32)
    glines = pltpu.VMEM((GLINES, BS), F32)
    grid = pltpu.VMEM((W, HL * BS), F32)
    shape = jax.ShapeDtypeStruct
    results = (
        shape((1, HL, W, BS), BF16),
        shape((2, BS, BS), F32),
        shape((2, BS), F32),
        shape((2, BS, BS), F32),
        shape((2, BS), F32),
        shape((1, BS), F32),
        shape((1, BS), F32),
    )
    in_vmem = pl.BlockSpec(memory_space=pltpu.VMEM)
    in_hbm = pl.BlockSpec(memory_space=pltpu.HBM)
    outs = pl.pallas_call(
        kernel,
        out_shape=tuple(pltpu.VMEM(r.shape, r.dtype) for r in results),
        in_specs=[in_hbm] * 12,
        out_specs=(in_vmem,) * 7,
        scratch_shapes=[
            lines, lines, lines, lines, lines, lines,
            pltpu.VMEM((2, SLINES, BS), F32), pltpu.VMEM((XS + 1, SLINES, BS), F32),
            pltpu.VMEM((SLINES, BS), F32), pltpu.VMEM((CHANS, SLINES, BS), F32),
            grid, grid, grid,
            pltpu.VMEM((2, 2 * BS, 2 * BS), F32),
            pltpu.VMEM((CORES, GLINES, BS), F32), glines, glines, glines,
            pltpu.VMEM((8 * PIECE, BS), F32), pltpu.VMEM((PIECE, BS), F32),
            pltpu.VMEM((CORES, GLINES, BS), F32),
            pltpu.SemaphoreType.DMA((SEMS,)),
            pltpu.SemaphoreType.DMA((SEMS,)),
            pltpu.SemaphoreType.DMA((12,)),
        ]
        + [pltpu.VMEM(source.shape, source.dtype) for source in sources],
        compiler_params=pltpu.CompilerParams(
            collective_id=0, has_side_effects=True, vmem_limit_bytes=60 * 1024 * 1024
        ),
    )(*sources)
    outs = pl.pallas_call(
        hand_out,
        out_shape=results,
        in_specs=[in_vmem] * 7,
        out_specs=(in_hbm,) * 7,
        scratch_shapes=[pltpu.SemaphoreType.DMA((7,))],
    )(*[pltpu.with_memory_space_constraint(o, pltpu.VMEM) for o in outs])
    return tuple(outs[:5]) + (outs[5].reshape(BS), outs[6].reshape(BS))


def solution(mesh):
    placed = (
        P(None, "row", None, "chan"),
        P(None, "row", None, "chan"),
        P("chan"),
        P("chan"),
        P(None, "chan", None),
        P(None, "chan"),
        P(None, "chan", None),
        P(None, "chan"),
    )
    return jax.shard_map(
        on_device,
        mesh=mesh,
        in_specs=placed,
        out_specs=(
            P(None, "row", None, "chan"),
            P(None, "chan", None),
            P(None, "chan"),
            P(None, "chan", None),
            P(None, "chan"),
            P("chan"),
            P("chan"),
        ),
        check_vma=False,
    )
```

```python
import math

import jax
import jax.numpy as jnp
import ml_dtypes
import numpy as np
from jax import lax
from jax.experimental import pallas as pl
from jax.experimental.pallas import tpu as pltpu
from jax.sharding import PartitionSpec as P

H = 192
W = 448
K = 192
BS = 128
C = 1024
ZS, YS, CORES = 8, 4, 2
ROWS = ZS * YS * CORES
CHIPS = ZS * YS
XS = 4
CHANS = 2 * XS
HL = H // ROWS
KL = K // ROWS
CHUNK = 2 * HL
LINES = ROWS * CHUNK
PIECE = 9
GLINES = CHIPS * PIECE
WT = -(-W // BS)
SLINES = 2 * HL * WT

EPS = 1e-05
LAMBDA = 0.01
ROOT_TWO_PI = math.sqrt(2.0 / math.pi)
F32 = jnp.float32
BF16 = jnp.bfloat16
MESH = pl.DeviceIdType.MESH
COT, MIXED, GRAD = 0, KL, 2 * KL
STATS, SUMS, SWAP, SCATTER, GATHER, JOIN = (3 * KL + i for i in (0, 2, 4, 5, 6, 7))
SEMS = 3 * KL + 8


def halves(table):
    table = table.astype(np.float32)
    high = table.astype(ml_dtypes.bfloat16)
    low = (table - high.astype(np.float32)).astype(ml_dtypes.bfloat16)
    return np.stack([high, low])


def lon_table():
    kk = np.arange(KL).reshape(KL, 1, 1)
    owner = np.arange(ROWS).reshape(1, ROWS, 1)
    part = np.arange(2).reshape(1, 1, 2)
    number, part = np.broadcast_arrays(owner * KL + kk, part)
    number, part = number.reshape(-1, 1), part.reshape(-1, 1)
    phase = (number * np.arange(W)[None, :] % W) * (2.0 * math.pi / W)
    return np.where(part == 0, np.cos(phase), -np.sin(phase)) / math.sqrt(W)


def lat_table():
    q = np.arange(2).reshape(2, 1, 1, 1, 1)
    g = np.arange(H).reshape(1, H, 1, 1, 1)
    hh = np.arange(HL).reshape(1, 1, HL, 1, 1)
    s = np.arange(ROWS).reshape(1, 1, 1, ROWS, 1)
    p = np.arange(2).reshape(1, 1, 1, 1, 2)
    phase = (g * (s * HL + hh) % H) * (2.0 * math.pi / H)
    cosine, sine = np.cos(phase), np.sin(phase)
    table = np.where(q == p, cosine, np.where(q == 0, sine, -sine)) / math.sqrt(H)
    return table.reshape(2 * H, HL * ROWS * 2)


def lon_back_table():
    table = halves(lon_table())[0].reshape(KL, 2 * ROWS, W).transpose(0, 2, 1)
    return np.concatenate([table, table], 2)


def dot(a, b):
    return lax.dot_general(a, b, (((1,), (0,)), ((), ())), preferred_element_type=F32)


def dot_t(a, b):
    return lax.dot_general(a, b, (((1,), (1,)), ((), ())), preferred_element_type=F32)


def dot_c(a, b):
    return lax.dot_general(a, b, (((0,), (0,)), ((), ())), preferred_element_type=F32)


def split(values):
    high = values.astype(BF16)
    return high, (values - high.astype(F32)).astype(BF16)


def dot3(table_high, table_low, values):
    high, low = split(values)
    return dot(table_high, high) + (dot(table_low, high) + dot(table_high, low))


def dot2(table, values):
    high, low = split(values)
    both = dot(table, jnp.concatenate([high, low], 1))
    width = values.shape[1]
    return both[:, :width] + both[:, width:]


def gelu_parts(values):
    square = values * values
    tangent = jnp.tanh(ROOT_TWO_PI * (values + 0.044715 * (square * values)))
    plus = 0.5 * (1.0 + tangent)
    slope = plus + 0.5 * values * (1.0 - tangent * tangent) * (
        ROOT_TWO_PI * (1.0 + 3.0 * 0.044715 * square)
    )
    return values * plus, slope


def block_matrix(weight):
    real, imag = weight[0], weight[1]
    return jnp.concatenate(
        [jnp.concatenate([real, imag], 1), jnp.concatenate([-imag, real], 1)], 0
    )


def diagonal(rows):
    return (
        lax.broadcasted_iota(jnp.int32, (rows, BS), 0)
        == lax.broadcasted_iota(jnp.int32, (rows, BS), 1)
    )


def pack(values):
    lines = []
    for t in range(WT):
        block = values[t * BS : min((t + 1) * BS, W)]
        lines.append(jnp.sum(jnp.where(diagonal(block.shape[0]), block, 0.0), 0, keepdims=True))
    return jnp.concatenate(lines, 0)


def spread(turned, line):
    blocks = []
    for t in range(WT):
        column = turned[: min(BS, W - t * BS), line + t : line + t + 1]
        blocks.append(jnp.broadcast_to(column, (column.shape[0], BS)))
    return jnp.concatenate(blocks, 0)


def kernel(*refs):
    sources, refs = refs[:12], refs[12:]
    held, refs = refs[-12:], refs[:-12]
    on_chip(sources, held, *held, *refs)


def on_chip(
    sources, held,
    cot_ref, lon_ref, x_ref, gain_ref, shift_ref, w1_ref, b1_ref, w2_ref, b2_ref,
    lat_ref, latt_ref, lont_ref,
    out_ref, gw1_ref, gb1_ref, gw2_ref, gb2_ref, gg_ref, gs_ref,
    sc, rc, sx, rx, sg, rg, st, rt, su, ru, normed_ref, rstd_ref, grad_ref, cot_spec_ref,
    dw_ref, gw, gx, hw, rw, fold, piece, aw,
    send_sem, recv_sem, load_sem,
):
    chan = lax.axis_index("chan")
    row = lax.axis_index("row")
    z, y, core = row // (YS * CORES), row // CORES % YS, row % CORES
    chip = row // CORES
    along_x = chan % XS
    chan_base = chan - along_x
    opposite = lax.rem(chan + XS, CHANS)
    twin = row + 1 - 2 * core

    ahead = [lax.rem(z + i, ZS) for i in range(ZS)]
    row_of = [a * (YS * CORES) for a in ahead]
    chip_of = [a * YS for a in ahead]

    def each_row(act, steps=tuple(range(ZS))):
        def level(i, carry):
            base = lax.rem(y + i // CORES, YS) * CORES + lax.rem(core + i, CORES)
            for step in steps:
                act(row_of[step] + base)
            return carry

        for step in steps:
            if step:
                act(row_of[step] + y * CORES + core)
        lax.fori_loop(1, YS * CORES, level, 0)

    def each_chip(act):
        def level(i, carry):
            base = lax.rem(y + i, YS)
            for offset in chip_of:
                act(offset + base)
            return carry

        for offset in chip_of[1:]:
            act(offset + y)
        lax.fori_loop(1, YS, level, 0)

    def peer_x(i):
        return chan_base + lax.rem(along_x + i, XS)

    loads = [
        pltpu.make_async_copy(source, target, load_sem.at[i])
        for i, (source, target) in enumerate(zip(sources, held))
    ]
    for load in loads[:3]:
        load.start()
    barrier = pltpu.get_barrier_semaphore()

    def greet(name, other):
        pl.semaphore_signal(barrier, inc=1, device_id={name: other}, device_id_type=MESH)

    for i in range(1, CHANS):
        greet("chan", lax.rem(chan + i, CHANS))
    each_row(lambda other: greet("row", other), (4, 3, 5, 2, 6, 1, 7, 0))

    def remote(source, target, which, name, other):
        return pltpu.make_async_remote_copy(
            src_ref=source,
            dst_ref=target,
            send_sem=send_sem.at[which],
            recv_sem=recv_sem.at[which],
            device_id={name: other},
            device_id_type=MESH,
        )

    def arrived(target, which):
        pltpu.make_async_copy(target, target, recv_sem.at[which]).wait()

    def left(target, which):
        pltpu.make_async_copy(target, target, send_sem.at[which]).wait()

    own = pl.ds(row * CHUNK, CHUNK)
    own_piece = pl.ds(chip * PIECE, PIECE)

    def send_chunks(source, target, k, which):
        def one(other):
            block = source.at[k, pl.ds(other * CHUNK, CHUNK)]
            remote(block, target.at[k, own], which + k, "row", other).start()

        each_row(one)
        pltpu.make_async_copy(
            source.at[k, own], target.at[k, own], recv_sem.at[which + k]
        ).start()

    for load in loads[:2]:
        load.wait()
    cot_wide = jnp.concatenate([cot_ref[0, h] for h in range(HL)], 1)

    def transform(k, product):
        rows = pl.ds(k * 2 * ROWS, 2 * ROWS)
        return product(lon_ref[0, rows, :], lon_ref[1, rows, :])

    def lay(target, k, values):
        for h in range(HL):
            target[k, pl.ds(h, 2 * ROWS, stride=HL), :] = values[:, h * BS : (h + 1) * BS]

    def cot_lon(k):
        lay(sc, k, transform(k, lambda high, low: dot(high, cot_wide) + dot(low, cot_wide)))

    cot_lon(0)

    loads[2].wait()
    ones = jnp.ones((BS, BS), F32).astype(BF16)
    for h in range(HL):
        block = x_ref[0, h]
        amount = dot(block, ones)
        centred = block.astype(F32) - amount * (1.0 / BS)
        high, low = split(centred * centred)
        st[0, pl.ds(h * WT, WT), :] = pack(amount)
        st[0, pl.ds((HL + h) * WT, WT), :] = pack(dot(high, ones) + dot(low, ones))
    pl.semaphore_wait(barrier, ROWS - 1 + CHANS - 1)

    for i in range(1, XS):
        remote(st.at[0], rt.at[along_x], STATS, "chan", peer_x(i)).start()
    send_chunks(sc, rc, 0, COT)
    cot_lon(1)
    cot_lon(2)

    arrived(rt.at[pl.ds(0, XS - 1)], STATS)
    mine = st[0]

    def part(i):
        return jnp.where(along_x == i, mine, rt[i])

    parts = [part(i) for i in range(XS)]
    half = SLINES // 2
    amount = parts[0][:half] + parts[1][:half] + parts[2][:half] + parts[3][:half]
    squares = parts[0][half:] + parts[1][half:] + parts[2][half:] + parts[3][half:]
    average = amount * (1.0 / (XS * BS))
    for i in range(XS):
        away = parts[i][:half] * (1.0 / BS) - average
        squares = squares + BS * (away * away)
    st[1] = jnp.concatenate([amount, squares], 0)
    remote(st.at[1], rt.at[XS], STATS + 1, "chan", opposite).start()

    send_chunks(sc, rc, 1, COT)
    send_chunks(sc, rc, 2, COT)
    for load in loads[3:]:
        load.start()

    arrived(rt.at[XS], STATS + 1)
    amount_two = rt[XS, pl.ds(0, half), :]
    mean = (amount + amount_two) * (1.0 / C)
    away = average - mean
    away_two = amount_two * (1.0 / (XS * BS)) - mean
    squares = squares + rt[XS, pl.ds(half, half), :] + (XS * BS) * (
        away * away + away_two * away_two
    )
    rstd = lax.rsqrt(squares * (1.0 / C) + EPS)

    turned = jnp.concatenate([mean, rstd], 0).T
    for h in range(HL):
        scale = spread(turned, half + h * WT)
        normed_ref[:, h * BS : (h + 1) * BS] = (
            x_ref[0, h].astype(F32) - spread(turned, h * WT)
        ) * scale
        rstd_ref[:, h * BS : (h + 1) * BS] = scale
    high, low = split(normed_ref[...])

    def mixed_lon(k):
        lay(sx, k, transform(k, lambda a, b: dot(a, high) + (dot(b, high) + dot(a, low))))

    mixed_lon(0)
    send_chunks(sx, rx, 0, MIXED)
    mixed_lon(1)
    send_chunks(sx, rx, 1, MIXED)
    mixed_lon(2)
    send_chunks(sx, rx, 2, MIXED)

    for load in loads[3:]:
        load.wait()
    one_matrix = block_matrix(w1_ref)
    two_matrix = block_matrix(w2_ref)
    one_bias = jnp.concatenate([b1_ref[0:1], b1_ref[1:2]], 1)
    two_bias = jnp.concatenate([b2_ref[0:1], b2_ref[1:2]], 1)
    gain = gain_ref[...]
    gain_two = jnp.concatenate([gain, gain], 1)
    shift_two = jnp.concatenate([shift_ref[...] * math.sqrt(H * W), jnp.zeros((1, BS), F32)], 1)
    first = jnp.where(row == 0, 1.0, 0.0).astype(F32)
    spec_scale = 1.0 / math.sqrt(H * K)
    ln_scale = 1.0 / math.sqrt(H * W)

    def gathered(landed, k):
        return jnp.concatenate(
            [landed[k, pl.ds(h, 2 * ROWS, stride=HL), :] for h in range(HL)], 0
        )

    def tokens(values):
        return jnp.concatenate([values[:H], values[H:]], 1)

    gain_sum = jnp.zeros((1, 2 * BS), F32)
    one_sum = jnp.zeros((1, 2 * BS), F32)
    two_sum = jnp.zeros((1, 2 * BS), F32)
    for k in range(KL):
        arrived(rc.at[k], COT + k)
    cot_spec = dot3(
        lat_ref[0], lat_ref[1], jnp.concatenate([gathered(rc, k) for k in range(KL)], 1)
    )
    for k in range(KL):
        block = tokens(cot_spec[:, k * BS : (k + 1) * BS])
        cot_spec_ref[k] = block * (2.0 - first if k == 0 else 2.0)
    for k in range(KL):
        arrived(rx.at[k], MIXED + k)
        values = gathered(rx, k)
        plain = tokens(dot2(lat_ref[0], values) + dot(lat_ref[1], values.astype(BF16)))
        mixed = plain * gain_two
        if k == 0:
            line = lax.broadcasted_iota(jnp.int32, (H, 2 * BS), 0)
            mixed = mixed + jnp.where(line == 0, shift_two * first, 0.0)
        rounded = mixed.astype(BF16)
        act, slope = gelu_parts(dot(rounded, one_matrix) + one_bias)
        hidden = act.astype(BF16)
        tangent = jnp.tanh((dot(hidden, two_matrix) + two_bias) * (1.0 / LAMBDA))
        grad_two = (cot_spec_ref[k] * (tangent * tangent)).astype(BF16)
        grad_pre = (dot_t(grad_two, two_matrix) * slope).astype(BF16)
        grad_spec = dot_t(grad_pre, one_matrix)
        grad_lat = dot2(
            latt_ref[...], jnp.concatenate([grad_spec[:, :BS], grad_spec[:, BS:]], 0)
        )
        for h in range(HL):
            sg[k, pl.ds(h, 2 * ROWS, stride=HL), :] = grad_lat[h * 2 * ROWS : (h + 1) * 2 * ROWS]
        if k < KL - 1:
            send_chunks(sg, rg, k, GRAD)
        two_sum = two_sum + jnp.sum(grad_two.astype(F32), 0, keepdims=True)
        one_sum = one_sum + jnp.sum(grad_pre.astype(F32), 0, keepdims=True)
        gain_sum = gain_sum + jnp.sum(grad_spec * plain, 0, keepdims=True)
        if k == 0:
            shift_sum = grad_spec[0:1, :BS] * first
        for layer, (before, after) in enumerate(((rounded, grad_pre), (hidden, grad_two))):
            product = dot_c(before, after)
            dw_ref[layer] = product if k == 0 else dw_ref[layer] + product

    for layer in range(2):
        product = dw_ref[layer] * spec_scale
        real = product[:BS, :BS] + product[BS:, BS:]
        imag = product[:BS, BS:] - product[BS:, :BS]
        for part_index, values in enumerate((real, imag)):
            for c in range(CORES):
                for sub in range(2):
                    start = (c * 2 + sub) * CHIPS
                    gw[c, pl.ds(layer * 4 + part_index * 2 + sub, CHIPS, stride=PIECE), :] = (
                        values[start : start + CHIPS]
                    )
    gain_sum = (gain_sum[:, :BS] + gain_sum[:, BS:]) * ln_scale
    gw[0, pl.ds(PIECE - 1, CHIPS, stride=PIECE), :] = jnp.concatenate(
        [
            one_sum[:, :BS] * spec_scale,
            one_sum[:, BS:] * spec_scale,
            two_sum[:, :BS] * spec_scale,
            two_sum[:, BS:] * spec_scale,
            gain_sum,
            shift_sum,
            jnp.zeros((CHIPS - 6, BS), F32),
        ],
        0,
    )
    gw[1, pl.ds(PIECE - 1, CHIPS, stride=PIECE), :] = jnp.zeros((CHIPS, BS), F32)
    remote(gw.at[1 - core], gx, SWAP, "row", twin).start()
    arrived(gx, SWAP)
    hw[...] = gw[core] + gx[...]

    def scatter(other):
        block = hw.at[pl.ds(other * PIECE, PIECE)]
        remote(block, rw.at[own_piece], SCATTER, "row", other * CORES + core).start()

    each_chip(scatter)
    pltpu.make_async_copy(hw.at[own_piece], rw.at[own_piece], recv_sem.at[SCATTER]).start()
    send_chunks(sg, rg, KL - 1, GRAD)

    def lon_back(k):
        values = jnp.concatenate(
            [rg[k, pl.ds(h, 2 * ROWS, stride=HL), :] for h in range(HL)], 1
        )
        high, low = split(values)
        return dot(lont_ref[k], jnp.concatenate([high, low], 0))

    arrived(rg.at[0], GRAD)
    grad_ref[...] = lon_back(0)
    arrived(rg.at[1], GRAD + 1)
    grad_ref[...] = grad_ref[...] + lon_back(1)

    arrived(rw, SCATTER)
    slab = 8 * PIECE
    summed = rw[pl.ds(0, slab), :]
    for s in range(1, CHIPS // 8):
        summed = summed + rw[pl.ds(s * slab, slab), :]
    fold[...] = summed
    summed = fold[pl.ds(0, PIECE), :]
    for s in range(1, 8):
        summed = summed + fold[pl.ds(s * PIECE, PIECE), :]
    piece[...] = summed

    def gather(other):
        remote(piece, aw.at[core, own_piece], GATHER, "row", other * CORES + core).start()

    each_chip(gather)
    pltpu.make_async_copy(piece, aw.at[core, own_piece], recv_sem.at[GATHER]).start()

    arrived(rg.at[2], GRAD + 2)
    zeros = jnp.zeros((BS, BS), F32).astype(BF16)
    pair = jnp.concatenate(
        [jnp.concatenate([ones, zeros], 1), jnp.concatenate([zeros, ones], 1)], 0
    )
    gain_wide = jnp.concatenate([gain] * HL, 1)
    grad_ref[...] = (grad_ref[...] + lon_back(2)) * gain_wide
    for h in range(HL):
        grad_norm = grad_ref[:, h * BS : (h + 1) * BS]
        product = grad_norm * normed_ref[:, h * BS : (h + 1) * BS]
        sums = dot(jnp.concatenate([grad_norm.astype(BF16), product.astype(BF16)], 1), pair)
        su[pl.ds(h * WT, WT), :] = pack(sums[:, :BS])
        su[pl.ds((HL + h) * WT, WT), :] = pack(sums[:, BS:])
    for i in range(1, CHANS):
        remote(su, ru.at[chan], SUMS, "chan", lax.rem(chan + i, CHANS)).start()
    pltpu.make_async_copy(su, ru.at[chan], recv_sem.at[SUMS]).start()

    for h in range(HL):
        lanes = slice(h * BS, (h + 1) * BS)
        scale = rstd_ref[:, lanes]
        grad_ref[:, lanes] = cot_ref[0, h].astype(F32) + scale * grad_ref[:, lanes]
        normed_ref[:, lanes] = scale * normed_ref[:, lanes]

    arrived(aw.at[core], GATHER)
    remote(aw.at[core], aw.at[core], JOIN, "row", twin).start()

    arrived(ru, SUMS)
    total = ru[0]
    for i in range(1, CHANS):
        total = total + ru[i]
    turned = (total * (1.0 / C)).T
    for h in range(HL):
        lanes = slice(h * BS, (h + 1) * BS)
        out_ref[0, h] = (
            grad_ref[:, lanes]
            - rstd_ref[:, lanes] * spread(turned, h * WT)
            - normed_ref[:, lanes] * spread(turned, half + h * WT)
        ).astype(BF16)

    arrived(aw.at[1 - core], JOIN)
    for layer, target in enumerate((gw1_ref, gw2_ref)):
        for part_index in range(2):
            for c in range(CORES):
                for sub in range(2):
                    start = (c * 2 + sub) * CHIPS
                    target[part_index, start : start + CHIPS] = aw[
                        c, pl.ds(layer * 4 + part_index * 2 + sub, CHIPS, stride=PIECE), :
                    ]
    extras = aw[0, pl.ds(PIECE - 1, 8, stride=PIECE), :]
    gb1_ref[...] = extras[0:2]
    gb2_ref[...] = extras[2:4]
    gg_ref[...] = extras[4:5]
    gs_ref[...] = extras[5:6]

    left(rt.at[pl.ds(0, XS - 1)], STATS)
    left(rt.at[XS], STATS + 1)
    left(ru.at[pl.ds(0, CHANS - 1)], SUMS)
    for k in range(KL):
        for which in (COT, MIXED, GRAD):
            left(rc.at[0, pl.ds(0, LINES - CHUNK)], which + k)
    for which in (SWAP, JOIN):
        left(hw, which)
    for which in (SCATTER, GATHER):
        left(hw.at[pl.ds(0, GLINES - PIECE)], which)


def hand_out(*refs):
    sem = refs[14]
    copies = [pltpu.make_async_copy(refs[i], refs[7 + i], sem.at[i]) for i in range(7)]
    for copy in copies:
        copy.start()
    for copy in copies:
        copy.wait()


def on_device(
    inputs, cotangent, ln_gain, ln_shift, first_weight, first_bias, second_weight, second_bias
):
    lat = lat_table()
    lon, lat, latt, lont = (
        jnp.asarray(t)
        for t in (halves(lon_table()), halves(lat), halves(lat.T)[0], lon_back_table())
    )
    sources = (
        cotangent, lon, inputs, ln_gain.reshape(1, BS), ln_shift.reshape(1, BS),
        first_weight, first_bias, second_weight, second_bias, lat, latt, lont,
    )
    lines = pltpu.VMEM((KL, LINES, BS), F32)
    glines = pltpu.VMEM((GLINES, BS), F32)
    grid = pltpu.VMEM((W, HL * BS), F32)
    shape = jax.ShapeDtypeStruct
    results = (
        shape((1, HL, W, BS), BF16),
        shape((2, BS, BS), F32),
        shape((2, BS), F32),
        shape((2, BS, BS), F32),
        shape((2, BS), F32),
        shape((1, BS), F32),
        shape((1, BS), F32),
    )
    in_vmem = pl.BlockSpec(memory_space=pltpu.VMEM)
    in_hbm = pl.BlockSpec(memory_space=pltpu.HBM)
    outs = pl.pallas_call(
        kernel,
        out_shape=tuple(pltpu.VMEM(r.shape, r.dtype) for r in results),
        in_specs=[in_hbm] * 12,
        out_specs=(in_vmem,) * 7,
        scratch_shapes=[
            lines, lines, lines, lines, lines, lines,
            pltpu.VMEM((2, SLINES, BS), F32), pltpu.VMEM((XS + 1, SLINES, BS), F32),
            pltpu.VMEM((SLINES, BS), F32), pltpu.VMEM((CHANS, SLINES, BS), F32),
            grid, grid, grid, pltpu.VMEM((KL, H, 2 * BS), F32),
            pltpu.VMEM((2, 2 * BS, 2 * BS), F32),
            pltpu.VMEM((CORES, GLINES, BS), F32), glines, glines, glines,
            pltpu.VMEM((8 * PIECE, BS), F32), pltpu.VMEM((PIECE, BS), F32),
            pltpu.VMEM((CORES, GLINES, BS), F32),
            pltpu.SemaphoreType.DMA((SEMS,)),
            pltpu.SemaphoreType.DMA((SEMS,)),
            pltpu.SemaphoreType.DMA((12,)),
        ]
        + [pltpu.VMEM(source.shape, source.dtype) for source in sources],
        compiler_params=pltpu.CompilerParams(
            collective_id=0, has_side_effects=True, vmem_limit_bytes=60 * 1024 * 1024
        ),
    )(*sources)
    outs = pl.pallas_call(
        hand_out,
        out_shape=results,
        in_specs=[in_vmem] * 7,
        out_specs=(in_hbm,) * 7,
        scratch_shapes=[pltpu.SemaphoreType.DMA((7,))],
    )(*[pltpu.with_memory_space_constraint(o, pltpu.VMEM) for o in outs])
    return tuple(outs[:5]) + (outs[5].reshape(BS), outs[6].reshape(BS))


def solution(mesh):
    placed = (
        P(None, "row", None, "chan"),
        P(None, "row", None, "chan"),
        P("chan"),
        P("chan"),
        P(None, "chan", None),
        P(None, "chan"),
        P(None, "chan", None),
        P(None, "chan"),
    )
    return jax.shard_map(
        on_device,
        mesh=mesh,
        in_specs=placed,
        out_specs=(
            P(None, "row", None, "chan"),
            P(None, "chan", None),
            P(None, "chan"),
            P(None, "chan", None),
            P(None, "chan"),
            P("chan"),
            P("chan"),
        ),
        check_vma=False,
    )
```

```python
import math

import jax
import jax.numpy as jnp
import ml_dtypes
import numpy as np
from jax import lax
from jax.experimental import pallas as pl
from jax.experimental.pallas import tpu as pltpu
from jax.sharding import PartitionSpec as P

H = 192
W = 448
K = 192
BS = 128
C = 1024
ZS, YS, CORES = 8, 4, 2
ROWS = ZS * YS * CORES
CHIPS = ZS * YS
XS = 4
CHANS = 2 * XS
HL = H // ROWS
KL = K // ROWS
CHUNK = 2 * HL
LINES = ROWS * CHUNK
PIECE = 9
GLINES = CHIPS * PIECE
WT = -(-W // BS)
SLINES = 2 * HL * WT

EPS = 1e-05
LAMBDA = 0.01
ROOT_TWO_PI = math.sqrt(2.0 / math.pi)
F32 = jnp.float32
BF16 = jnp.bfloat16
MESH = pl.DeviceIdType.MESH
COT, MIXED, GRAD = 0, KL, 2 * KL
STATS, SUMS, SWAP, SCATTER, GATHER, JOIN = (3 * KL + i for i in (0, 2, 4, 5, 6, 7))
SEMS = 3 * KL + 8


def halves(table):
    table = table.astype(np.float32)
    high = table.astype(ml_dtypes.bfloat16)
    low = (table - high.astype(np.float32)).astype(ml_dtypes.bfloat16)
    return np.stack([high, low])


def lon_table():
    kk = np.arange(KL).reshape(KL, 1, 1)
    owner = np.arange(ROWS).reshape(1, ROWS, 1)
    part = np.arange(2).reshape(1, 1, 2)
    number, part = np.broadcast_arrays(owner * KL + kk, part)
    number, part = number.reshape(-1, 1), part.reshape(-1, 1)
    phase = (number * np.arange(W)[None, :] % W) * (2.0 * math.pi / W)
    return np.where(part == 0, np.cos(phase), -np.sin(phase)) / math.sqrt(W)


def lat_table():
    q = np.arange(2).reshape(2, 1, 1, 1, 1)
    g = np.arange(H).reshape(1, H, 1, 1, 1)
    hh = np.arange(HL).reshape(1, 1, HL, 1, 1)
    s = np.arange(ROWS).reshape(1, 1, 1, ROWS, 1)
    p = np.arange(2).reshape(1, 1, 1, 1, 2)
    phase = (g * (s * HL + hh) % H) * (2.0 * math.pi / H)
    cosine, sine = np.cos(phase), np.sin(phase)
    table = np.where(q == p, cosine, np.where(q == 0, sine, -sine)) / math.sqrt(H)
    return table.reshape(2 * H, HL * ROWS * 2)


def lon_back_table():
    table = halves(lon_table())[0].reshape(KL, 2 * ROWS, W).transpose(0, 2, 1)
    return np.concatenate([table, table], 2)


def dot(a, b):
    return lax.dot_general(a, b, (((1,), (0,)), ((), ())), preferred_element_type=F32)


def dot_t(a, b):
    return lax.dot_general(a, b, (((1,), (1,)), ((), ())), preferred_element_type=F32)


def dot_c(a, b):
    return lax.dot_general(a, b, (((0,), (0,)), ((), ())), preferred_element_type=F32)


def split(values):
    high = values.astype(BF16)
    return high, (values - high.astype(F32)).astype(BF16)


def dot3(table_high, table_low, values):
    high, low = split(values)
    return dot(table_high, high) + (dot(table_low, high) + dot(table_high, low))


def dot2(table, values):
    high, low = split(values)
    both = dot(table, jnp.concatenate([high, low], 1))
    width = values.shape[1]
    return both[:, :width] + both[:, width:]


def gelu_parts(values):
    square = values * values
    tangent = jnp.tanh(ROOT_TWO_PI * (values + 0.044715 * (square * values)))
    plus = 0.5 * (1.0 + tangent)
    slope = plus + 0.5 * values * (1.0 - tangent * tangent) * (
        ROOT_TWO_PI * (1.0 + 3.0 * 0.044715 * square)
    )
    return values * plus, slope


def block_matrix(weight):
    real, imag = weight[0], weight[1]
    return jnp.concatenate(
        [jnp.concatenate([real, imag], 1), jnp.concatenate([-imag, real], 1)], 0
    )


def diagonal(rows):
    return (
        lax.broadcasted_iota(jnp.int32, (rows, BS), 0)
        == lax.broadcasted_iota(jnp.int32, (rows, BS), 1)
    )


def pack(values):
    lines = []
    for t in range(WT):
        block = values[t * BS : min((t + 1) * BS, W)]
        lines.append(jnp.sum(jnp.where(diagonal(block.shape[0]), block, 0.0), 0, keepdims=True))
    return jnp.concatenate(lines, 0)


def spread(turned, line):
    blocks = []
    for t in range(WT):
        column = turned[: min(BS, W - t * BS), line + t : line + t + 1]
        blocks.append(jnp.broadcast_to(column, (column.shape[0], BS)))
    return jnp.concatenate(blocks, 0)


def kernel(*refs):
    sources, refs = refs[:12], refs[12:]
    held, refs = refs[-12:], refs[:-12]
    on_chip(sources, held, *held, *refs)


def on_chip(
    sources, held,
    cot_ref, lon_ref, x_ref, gain_ref, shift_ref, w1_ref, b1_ref, w2_ref, b2_ref,
    lat_ref, latt_ref, lont_ref,
    out_ref, gw1_ref, gb1_ref, gw2_ref, gb2_ref, gg_ref, gs_ref,
    sc, rc, sx, rx, sg, rg, st, rt, su, ru, normed_ref, rstd_ref, grad_ref, cot_spec_ref,
    dw_ref, gw, gx, hw, rw, fold, piece, aw,
    send_sem, recv_sem, load_sem,
):
    chan = lax.axis_index("chan")
    row = lax.axis_index("row")
    z, y, core = row // (YS * CORES), row // CORES % YS, row % CORES
    chip = row // CORES
    along_x = chan % XS
    chan_base = chan - along_x
    opposite = lax.rem(chan + XS, CHANS)
    twin = row + 1 - 2 * core

    ahead = [lax.rem(z + i, ZS) for i in range(ZS)]
    row_of = [a * (YS * CORES) for a in ahead]
    chip_of = [a * YS for a in ahead]

    def each_row(act, steps=tuple(range(ZS))):
        def level(i, carry):
            base = lax.rem(y + i // CORES, YS) * CORES + lax.rem(core + i, CORES)
            for step in steps:
                act(row_of[step] + base)
            return carry

        for step in steps:
            if step:
                act(row_of[step] + y * CORES + core)
        lax.fori_loop(1, YS * CORES, level, 0)

    def each_chip(act):
        def level(i, carry):
            base = lax.rem(y + i, YS)
            for offset in chip_of:
                act(offset + base)
            return carry

        for offset in chip_of[1:]:
            act(offset + y)
        lax.fori_loop(1, YS, level, 0)

    def peer_x(i):
        return chan_base + lax.rem(along_x + i, XS)

    loads = [
        pltpu.make_async_copy(source, target, load_sem.at[i])
        for i, (source, target) in enumerate(zip(sources, held))
    ]
    for load in loads[:3]:
        load.start()
    barrier = pltpu.get_barrier_semaphore()

    def greet(name, other):
        pl.semaphore_signal(barrier, inc=1, device_id={name: other}, device_id_type=MESH)

    for i in range(1, CHANS):
        greet("chan", lax.rem(chan + i, CHANS))
    each_row(lambda other: greet("row", other), (4, 3, 5, 2, 6, 1, 7, 0))

    def remote(source, target, which, name, other):
        return pltpu.make_async_remote_copy(
            src_ref=source,
            dst_ref=target,
            send_sem=send_sem.at[which],
            recv_sem=recv_sem.at[which],
            device_id={name: other},
            device_id_type=MESH,
        )

    def arrived(target, which):
        pltpu.make_async_copy(target, target, recv_sem.at[which]).wait()

    def left(target, which):
        pltpu.make_async_copy(target, target, send_sem.at[which]).wait()

    own = pl.ds(row * CHUNK, CHUNK)
    own_piece = pl.ds(chip * PIECE, PIECE)

    def send_chunks(source, target, k, which):
        def one(other):
            block = source.at[k, pl.ds(other * CHUNK, CHUNK)]
            remote(block, target.at[k, own], which + k, "row", other).start()

        each_row(one)
        pltpu.make_async_copy(
            source.at[k, own], target.at[k, own], recv_sem.at[which + k]
        ).start()

    for load in loads[:2]:
        load.wait()
    cot_wide = jnp.concatenate([cot_ref[0, h] for h in range(HL)], 1)

    def transform(k, product):
        rows = pl.ds(k * 2 * ROWS, 2 * ROWS)
        return product(lon_ref[0, rows, :], lon_ref[1, rows, :])

    def lay(target, k, values):
        for h in range(HL):
            target[k, pl.ds(h, 2 * ROWS, stride=HL), :] = values[:, h * BS : (h + 1) * BS]

    def cot_lon(k):
        lay(sc, k, transform(k, lambda high, low: dot(high, cot_wide) + dot(low, cot_wide)))

    cot_lon(0)

    loads[2].wait()
    ones = jnp.ones((BS, BS), F32).astype(BF16)
    for h in range(HL):
        block = x_ref[0, h]
        amount = dot(block, ones)
        centred = block.astype(F32) - amount * (1.0 / BS)
        high, low = split(centred * centred)
        st[0, pl.ds(h * WT, WT), :] = pack(amount)
        st[0, pl.ds((HL + h) * WT, WT), :] = pack(dot(high, ones) + dot(low, ones))
    pl.semaphore_wait(barrier, ROWS - 1 + CHANS - 1)

    for i in range(1, XS):
        remote(st.at[0], rt.at[along_x], STATS, "chan", peer_x(i)).start()
    send_chunks(sc, rc, 0, COT)
    cot_lon(1)
    cot_lon(2)

    arrived(rt.at[pl.ds(0, XS - 1)], STATS)
    mine = st[0]

    def part(i):
        return jnp.where(along_x == i, mine, rt[i])

    parts = [part(i) for i in range(XS)]
    half = SLINES // 2
    amount = parts[0][:half] + parts[1][:half] + parts[2][:half] + parts[3][:half]
    squares = parts[0][half:] + parts[1][half:] + parts[2][half:] + parts[3][half:]
    average = amount * (1.0 / (XS * BS))
    for i in range(XS):
        away = parts[i][:half] * (1.0 / BS) - average
        squares = squares + BS * (away * away)
    st[1] = jnp.concatenate([amount, squares], 0)
    remote(st.at[1], rt.at[XS], STATS + 1, "chan", opposite).start()

    send_chunks(sc, rc, 1, COT)
    send_chunks(sc, rc, 2, COT)
    for load in loads[3:]:
        load.start()

    arrived(rt.at[XS], STATS + 1)
    amount_two = rt[XS, pl.ds(0, half), :]
    mean = (amount + amount_two) * (1.0 / C)
    away = average - mean
    away_two = amount_two * (1.0 / (XS * BS)) - mean
    squares = squares + rt[XS, pl.ds(half, half), :] + (XS * BS) * (
        away * away + away_two * away_two
    )
    rstd = lax.rsqrt(squares * (1.0 / C) + EPS)

    turned = jnp.concatenate([mean, rstd], 0).T
    for h in range(HL):
        scale = spread(turned, half + h * WT)
        normed_ref[:, h * BS : (h + 1) * BS] = (
            x_ref[0, h].astype(F32) - spread(turned, h * WT)
        ) * scale
        rstd_ref[:, h * BS : (h + 1) * BS] = scale
    high, low = split(normed_ref[...])

    def mixed_lon(k):
        lay(sx, k, transform(k, lambda a, b: dot(a, high) + (dot(b, high) + dot(a, low))))

    mixed_lon(0)
    send_chunks(sx, rx, 0, MIXED)
    mixed_lon(1)
    send_chunks(sx, rx, 1, MIXED)
    mixed_lon(2)
    send_chunks(sx, rx, 2, MIXED)

    for load in loads[3:]:
        load.wait()
    one_matrix = block_matrix(w1_ref)
    two_matrix = block_matrix(w2_ref)
    one_bias = jnp.concatenate([b1_ref[0:1], b1_ref[1:2]], 1)
    two_bias = jnp.concatenate([b2_ref[0:1], b2_ref[1:2]], 1)
    gain = gain_ref[...]
    gain_two = jnp.concatenate([gain, gain], 1)
    shift_two = jnp.concatenate([shift_ref[...] * math.sqrt(H * W), jnp.zeros((1, BS), F32)], 1)
    first = jnp.where(row == 0, 1.0, 0.0).astype(F32)
    spec_scale = 1.0 / math.sqrt(H * K)
    ln_scale = 1.0 / math.sqrt(H * W)

    def gathered(landed, k):
        return jnp.concatenate(
            [landed[k, pl.ds(h, 2 * ROWS, stride=HL), :] for h in range(HL)], 0
        )

    def tokens(values):
        return jnp.concatenate([values[:H], values[H:]], 1)

    def back(k, values):
        values = dot2(latt_ref[...], jnp.concatenate([values[:, :BS], values[:, BS:]], 0))
        for h in range(HL):
            sg[k, pl.ds(h, 2 * ROWS, stride=HL), :] = values[h * 2 * ROWS : (h + 1) * 2 * ROWS]

    gain_sum = jnp.zeros((1, 2 * BS), F32)
    one_sum = jnp.zeros((1, 2 * BS), F32)
    two_sum = jnp.zeros((1, 2 * BS), F32)
    for k in range(KL):
        arrived(rc.at[k], COT + k)
    cot_spec = dot3(
        lat_ref[0], lat_ref[1], jnp.concatenate([gathered(rc, k) for k in range(KL)], 1)
    )
    for k in range(KL):
        block = tokens(cot_spec[:, k * BS : (k + 1) * BS])
        cot_spec_ref[k] = block * (2.0 - first if k == 0 else 2.0)
    for k in range(KL):
        arrived(rx.at[k], MIXED + k)
        values = gathered(rx, k)
        plain = tokens(dot2(lat_ref[0], values) + dot(lat_ref[1], values.astype(BF16)))
        mixed = plain * gain_two
        if k == 0:
            line = lax.broadcasted_iota(jnp.int32, (H, 2 * BS), 0)
            mixed = mixed + jnp.where(line == 0, shift_two * first, 0.0)
        rounded = mixed.astype(BF16)
        act, slope = gelu_parts(dot(rounded, one_matrix) + one_bias)
        hidden = act.astype(BF16)
        tangent = jnp.tanh((dot(hidden, two_matrix) + two_bias) * (1.0 / LAMBDA))
        grad_two = (cot_spec_ref[k] * (tangent * tangent)).astype(BF16)
        grad_pre = (dot_t(grad_two, two_matrix) * slope).astype(BF16)
        grad_spec = dot_t(grad_pre, one_matrix)
        if k < KL - 1:
            back(k, grad_spec)
            send_chunks(sg, rg, k, GRAD)
        two_sum = two_sum + jnp.sum(grad_two.astype(F32), 0, keepdims=True)
        one_sum = one_sum + jnp.sum(grad_pre.astype(F32), 0, keepdims=True)
        gain_sum = gain_sum + jnp.sum(grad_spec * plain, 0, keepdims=True)
        if k == 0:
            shift_sum = grad_spec[0:1, :BS] * first
        for layer, (before, after) in enumerate(((rounded, grad_pre), (hidden, grad_two))):
            product = dot_c(before, after)
            dw_ref[layer] = product if k == 0 else dw_ref[layer] + product

    for layer in range(2):
        product = dw_ref[layer] * spec_scale
        real = product[:BS, :BS] + product[BS:, BS:]
        imag = product[:BS, BS:] - product[BS:, :BS]
        for part_index, values in enumerate((real, imag)):
            for c in range(CORES):
                for sub in range(2):
                    start = (c * 2 + sub) * CHIPS
                    gw[c, pl.ds(layer * 4 + part_index * 2 + sub, CHIPS, stride=PIECE), :] = (
                        values[start : start + CHIPS]
                    )
    gain_sum = (gain_sum[:, :BS] + gain_sum[:, BS:]) * ln_scale
    gw[0, pl.ds(PIECE - 1, CHIPS, stride=PIECE), :] = jnp.concatenate(
        [
            one_sum[:, :BS] * spec_scale,
            one_sum[:, BS:] * spec_scale,
            two_sum[:, :BS] * spec_scale,
            two_sum[:, BS:] * spec_scale,
            gain_sum,
            shift_sum,
            jnp.zeros((CHIPS - 6, BS), F32),
        ],
        0,
    )
    gw[1, pl.ds(PIECE - 1, CHIPS, stride=PIECE), :] = jnp.zeros((CHIPS, BS), F32)
    remote(gw.at[1 - core], gx, SWAP, "row", twin).start()
    back(KL - 1, grad_spec)
    arrived(gx, SWAP)
    hw[...] = gw[core] + gx[...]

    def scatter(other):
        block = hw.at[pl.ds(other * PIECE, PIECE)]
        remote(block, rw.at[own_piece], SCATTER, "row", other * CORES + core).start()

    each_chip(scatter)
    pltpu.make_async_copy(hw.at[own_piece], rw.at[own_piece], recv_sem.at[SCATTER]).start()
    send_chunks(sg, rg, KL - 1, GRAD)

    def lon_back(k):
        values = jnp.concatenate(
            [rg[k, pl.ds(h, 2 * ROWS, stride=HL), :] for h in range(HL)], 1
        )
        high, low = split(values)
        return dot(lont_ref[k], jnp.concatenate([high, low], 0))

    arrived(rg.at[0], GRAD)
    grad_ref[...] = lon_back(0)
    arrived(rg.at[1], GRAD + 1)
    grad_ref[...] = grad_ref[...] + lon_back(1)

    arrived(rw, SCATTER)
    slab = 8 * PIECE
    summed = rw[pl.ds(0, slab), :]
    for s in range(1, CHIPS // 8):
        summed = summed + rw[pl.ds(s * slab, slab), :]
    fold[...] = summed
    summed = fold[pl.ds(0, PIECE), :]
    for s in range(1, 8):
        summed = summed + fold[pl.ds(s * PIECE, PIECE), :]
    piece[...] = summed

    def gather(other):
        remote(piece, aw.at[core, own_piece], GATHER, "row", other * CORES + core).start()

    each_chip(gather)
    pltpu.make_async_copy(piece, aw.at[core, own_piece], recv_sem.at[GATHER]).start()

    arrived(rg.at[2], GRAD + 2)
    zeros = jnp.zeros((BS, BS), F32).astype(BF16)
    pair = jnp.concatenate(
        [jnp.concatenate([ones, zeros], 1), jnp.concatenate([zeros, ones], 1)], 0
    )
    gain_wide = jnp.concatenate([gain] * HL, 1)
    grad_ref[...] = (grad_ref[...] + lon_back(2)) * gain_wide
    for h in range(HL):
        grad_norm = grad_ref[:, h * BS : (h + 1) * BS]
        product = grad_norm * normed_ref[:, h * BS : (h + 1) * BS]
        sums = dot(jnp.concatenate([grad_norm.astype(BF16), product.astype(BF16)], 1), pair)
        su[pl.ds(h * WT, WT), :] = pack(sums[:, :BS])
        su[pl.ds((HL + h) * WT, WT), :] = pack(sums[:, BS:])
    for i in range(1, CHANS):
        remote(su, ru.at[chan], SUMS, "chan", lax.rem(chan + i, CHANS)).start()
    pltpu.make_async_copy(su, ru.at[chan], recv_sem.at[SUMS]).start()

    for h in range(HL):
        lanes = slice(h * BS, (h + 1) * BS)
        scale = rstd_ref[:, lanes]
        grad_ref[:, lanes] = cot_ref[0, h].astype(F32) + scale * grad_ref[:, lanes]
        normed_ref[:, lanes] = scale * normed_ref[:, lanes]

    arrived(aw.at[core], GATHER)
    remote(aw.at[core], aw.at[core], JOIN, "row", twin).start()

    arrived(ru, SUMS)
    total = ru[0]
    for i in range(1, CHANS):
        total = total + ru[i]
    turned = (total * (1.0 / C)).T
    for h in range(HL):
        lanes = slice(h * BS, (h + 1) * BS)
        out_ref[0, h] = (
            grad_ref[:, lanes]
            - rstd_ref[:, lanes] * spread(turned, h * WT)
            - normed_ref[:, lanes] * spread(turned, half + h * WT)
        ).astype(BF16)

    arrived(aw.at[1 - core], JOIN)
    for layer, target in enumerate((gw1_ref, gw2_ref)):
        for part_index in range(2):
            for c in range(CORES):
                for sub in range(2):
                    start = (c * 2 + sub) * CHIPS
                    target[part_index, start : start + CHIPS] = aw[
                        c, pl.ds(layer * 4 + part_index * 2 + sub, CHIPS, stride=PIECE), :
                    ]
    extras = aw[0, pl.ds(PIECE - 1, 8, stride=PIECE), :]
    gb1_ref[...] = extras[0:2]
    gb2_ref[...] = extras[2:4]
    gg_ref[...] = extras[4:5]
    gs_ref[...] = extras[5:6]

    left(rt.at[pl.ds(0, XS - 1)], STATS)
    left(rt.at[XS], STATS + 1)
    left(ru.at[pl.ds(0, CHANS - 1)], SUMS)
    for k in range(KL):
        for which in (COT, MIXED, GRAD):
            left(rc.at[0, pl.ds(0, LINES - CHUNK)], which + k)
    for which in (SWAP, JOIN):
        left(hw, which)
    for which in (SCATTER, GATHER):
        left(hw.at[pl.ds(0, GLINES - PIECE)], which)


def hand_out(*refs):
    sem = refs[14]
    pairs = [(refs[i], refs[7 + i]) for i in range(1, 7)]
    for h in range(HL):
        for start in range(0, W, W // 2):
            rows = pl.ds(start, W // 2)
            pairs.insert(0, (refs[0].at[0, h, rows], refs[7].at[0, h, rows]))
    copies = [
        pltpu.make_async_copy(source, target, sem.at[i])
        for i, (source, target) in enumerate(pairs)
    ]
    for copy in copies:
        copy.start()
    for copy in copies:
        copy.wait()


def on_device(
    inputs, cotangent, ln_gain, ln_shift, first_weight, first_bias, second_weight, second_bias
):
    lat = lat_table()
    lon, lat, latt, lont = (
        jnp.asarray(t)
        for t in (halves(lon_table()), halves(lat), halves(lat.T)[0], lon_back_table())
    )
    sources = (
        cotangent, lon, inputs, ln_gain.reshape(1, BS), ln_shift.reshape(1, BS),
        first_weight, first_bias, second_weight, second_bias, lat, latt, lont,
    )
    lines = pltpu.VMEM((KL, LINES, BS), F32)
    glines = pltpu.VMEM((GLINES, BS), F32)
    grid = pltpu.VMEM((W, HL * BS), F32)
    shape = jax.ShapeDtypeStruct
    results = (
        shape((1, HL, W, BS), BF16),
        shape((2, BS, BS), F32),
        shape((2, BS), F32),
        shape((2, BS, BS), F32),
        shape((2, BS), F32),
        shape((1, BS), F32),
        shape((1, BS), F32),
    )
    in_vmem = pl.BlockSpec(memory_space=pltpu.VMEM)
    in_hbm = pl.BlockSpec(memory_space=pltpu.HBM)
    outs = pl.pallas_call(
        kernel,
        out_shape=tuple(pltpu.VMEM(r.shape, r.dtype) for r in results),
        in_specs=[in_hbm] * 12,
        out_specs=(in_vmem,) * 7,
        scratch_shapes=[
            lines, lines, lines, lines, lines, lines,
            pltpu.VMEM((2, SLINES, BS), F32), pltpu.VMEM((XS + 1, SLINES, BS), F32),
            pltpu.VMEM((SLINES, BS), F32), pltpu.VMEM((CHANS, SLINES, BS), F32),
            grid, grid, grid, pltpu.VMEM((KL, H, 2 * BS), F32),
            pltpu.VMEM((2, 2 * BS, 2 * BS), F32),
            pltpu.VMEM((CORES, GLINES, BS), F32), glines, glines, glines,
            pltpu.VMEM((8 * PIECE, BS), F32), pltpu.VMEM((PIECE, BS), F32),
            pltpu.VMEM((CORES, GLINES, BS), F32),
            pltpu.SemaphoreType.DMA((SEMS,)),
            pltpu.SemaphoreType.DMA((SEMS,)),
            pltpu.SemaphoreType.DMA((12,)),
        ]
        + [pltpu.VMEM(source.shape, source.dtype) for source in sources],
        compiler_params=pltpu.CompilerParams(
            collective_id=0, has_side_effects=True, vmem_limit_bytes=60 * 1024 * 1024
        ),
    )(*sources)
    outs = pl.pallas_call(
        hand_out,
        out_shape=results,
        in_specs=[in_vmem] * 7,
        out_specs=(in_hbm,) * 7,
        scratch_shapes=[pltpu.SemaphoreType.DMA((2 * HL + 6,))],
    )(*[pltpu.with_memory_space_constraint(o, pltpu.VMEM) for o in outs])
    return tuple(outs[:5]) + (outs[5].reshape(BS), outs[6].reshape(BS))


def solution(mesh):
    placed = (
        P(None, "row", None, "chan"),
        P(None, "row", None, "chan"),
        P("chan"),
        P("chan"),
        P(None, "chan", None),
        P(None, "chan"),
        P(None, "chan", None),
        P(None, "chan"),
    )
    return jax.shard_map(
        on_device,
        mesh=mesh,
        in_specs=placed,
        out_specs=(
            P(None, "row", None, "chan"),
            P(None, "chan", None),
            P(None, "chan"),
            P(None, "chan", None),
            P(None, "chan"),
            P("chan"),
            P("chan"),
        ),
        check_vma=False,
    )
```
